128 devices in a mesh: gz: 32 (over x, z, core), gy: 4 (over y).
Axes of the slice: x: 4, y: 4, z: 4, core: 2. Of those that a mesh axis runs over, the one named last changes fastest.
Arguments:
- features: bfloat16 [512, 64, 32, 128], P('gz', 'gy'), may hold values from -6 to 6
- occupancy: int32 [32, 4, 4], P('gz', 'gy'), may hold values from 0 to 1, as said below
- kernel: bfloat16 [3, 3, 3, 64, 128], replicated, may hold values from -0.15625 to 0.15625
- upstream: bfloat16 [256, 32, 32, 128], P('gz', 'gy'), may hold values from -6 to 6
Outputs:
- coarse: bfloat16 [256, 32, 32, 128], P('gz', 'gy')
- feature_grad: bfloat16 [512, 64, 32, 128], P('gz', 'gy')
- kernel_grad: float32 [3, 3, 3, 64, 128], replicated
The draws below stay inside these ranges and needn't reach their ends.
Inputs may be any that keep to these rules, and one draw needn't show every extreme that they name: `occupancy`: each owner of 1 x 1 x 4 blocks holds at least one occupied block; owners' blocks are occupied at their own rates, so occupied counts differ between devices.
All inputs are finite; a program needn't handle non-finite values.
Results may differ from the reference program's by a relative error of at most 0.0022.
Values may be sent and summed in bfloat16 or wider, within the bound.
A program may use at most 128 MiB of HBM per device.

```python
import jax
import jax.numpy as jnp
from jax import lax

C_IN = 64
C_OUT = 128
BE = 16
BZ = 1
BY = 1
BX = 4
NZ = 512
NY = 64
NX = 64


def draw_occupancy(key, part):
    owner_rows = NZ // BE // BZ
    owner_cols = NY // BE // BY
    rates = jax.random.randint(jax.random.fold_in(key, 11), (owner_rows, owner_cols, 1), 2, 9)
    rates = jnp.repeat(jnp.repeat(rates, BZ, axis=0), BY, axis=1)
    rolls = jax.random.randint(jax.random.fold_in(key, 12), (NZ // BE, NY // BE, BX), 0, 10)
    chosen = jax.random.randint(jax.random.fold_in(key, 13), (owner_rows, owner_cols, 1), 0, BX)
    chosen = jnp.repeat(jnp.repeat(chosen, BZ, axis=0), BY, axis=1)
    column = jnp.arange(BX, dtype=jnp.int32)[None, None, :]
    row_local = (jnp.arange(NZ // BE, dtype=jnp.int32) % BZ)[:, None, None]
    band_local = (jnp.arange(NY // BE, dtype=jnp.int32) % BY)[None, :, None]
    forced = (column == chosen) & (row_local == 0) & (band_local == 0)
    return ((rolls < rates) | forced).astype(jnp.int32)


def block_levels(key, extent, shards, low, high):
    factor_of = 1.0
    for dim, shards_of in shards:
        draws = jax.random.uniform(jax.random.fold_in(jax.random.fold_in(key, 6), dim), (shards_of,), jnp.float32, low / len(shards), high / len(shards))
        factor_of = factor_of * jnp.repeat(jnp.exp(draws), extent[dim] // shards_of).reshape((-1,) + (1,) * (len(extent) - 1 - dim))
    return factor_of


def centred(stream_key, dims, spread, reach, shards=(), kind=jnp.bfloat16):
    loudness = block_levels(stream_key, dims, shards, -0.22, 0.18) if shards else 1.0
    values = jax.random.normal(stream_key, dims, jnp.float32) * spread * loudness
    return jnp.minimum(jnp.maximum(values, -reach), reach).astype(kind)


def setup_inputs(seed: int = 0) -> dict:
    arg_keys = jax.random.split(jax.random.key(seed), 5)
    return {
        "features": centred(arg_keys[0], (NZ, NY, NX // 2, 2 * C_IN), 1.0, 6.0, ((0, 32), (1, 4))),
        "occupancy": draw_occupancy(jax.random.fold_in(arg_keys[4], 71), 0),
        "kernel": centred(arg_keys[2], (3, 3, 3, C_IN, C_OUT), (27 * C_IN) ** -0.5, 0.15625),
        "upstream": centred(arg_keys[3], (NZ // 2, NY // 2, NX // 2, C_OUT), 1.0, 6.0, ((0, 32), (1, 4))),
    }


def expand(mask, edge, xedge):
    full = jnp.repeat(mask, edge, axis=0)
    full = jnp.repeat(full, edge, axis=1)
    return jnp.repeat(full, xedge, axis=2)

def strided(ext, kz, ky, zo, yo):
    return lax.slice(ext, (kz, ky, 0, 0), (kz + 2 * zo - 1, ky + 2 * yo - 1, ext.shape[2], ext.shape[3]), (2, 2, 1, 1))

def shifted_odd(piece, cin):
    odd = piece[..., cin:]
    return jnp.concatenate([jnp.zeros_like(odd[:, :, :1]), odd[:, :, :-1]], 2)

def convolve(ext, kernel):
    zo = (ext.shape[0] - 1) // 2
    yo = (ext.shape[1] - 1) // 2
    pairs = ext.shape[2]
    cin = kernel.shape[3]
    cout = kernel.shape[4]
    total = jnp.zeros((zo * yo * pairs, cout), jnp.float32)
    for kz in range(3):
        for ky in range(3):
            piece = strided(ext, kz, ky, zo, yo)
            pair_w = jnp.concatenate([kernel[kz, ky, 1], kernel[kz, ky, 2]], 0)
            total = total + jnp.dot(piece.reshape(-1, 2 * cin), pair_w, preferred_element_type=jnp.float32)
            total = total + jnp.dot(shifted_odd(piece, cin).reshape(-1, cin), kernel[kz, ky, 0], preferred_element_type=jnp.float32)
    return total.reshape(zo, yo, pairs, cout)

def data_grad(kernel, grad):
    zo, yo, pairs, cout = grad.shape
    cin = kernel.shape[3]
    flat = grad.reshape(-1, cout)
    dext = jnp.zeros((2 * zo + 1, 2 * yo + 1, pairs, 2 * cin), jnp.float32)
    for kz in range(3):
        for ky in range(3):
            pair_w = jnp.concatenate([kernel[kz, ky, 1], kernel[kz, ky, 2]], 0)
            d_pair = jnp.dot(flat, pair_w.T, preferred_element_type=jnp.float32).reshape(zo, yo, pairs, 2 * cin)
            d_odd = jnp.dot(flat, kernel[kz, ky, 0].T, preferred_element_type=jnp.float32).reshape(zo, yo, pairs, cin)
            back = jnp.concatenate([d_odd[:, :, 1:], jnp.zeros_like(d_odd[:, :, :1])], 2)
            piece = d_pair + jnp.concatenate([jnp.zeros_like(back), back], 3)
            placed = lax.pad(piece, jnp.float32(0.0), ((kz, 2 - kz, 1), (ky, 2 - ky, 1), (0, 0, 0), (0, 0, 0)))
            dext = dext + placed
    return dext

def weight_grad(ext, grad, cin):
    zo, yo, pairs, cout = grad.shape
    flat = grad.reshape(-1, cout)
    parts_list = []
    for kz in range(3):
        for ky in range(3):
            piece = strided(ext, kz, ky, zo, yo)
            d_pair = jnp.dot(piece.reshape(-1, 2 * cin).T, flat, preferred_element_type=jnp.float32)
            d_odd = jnp.dot(shifted_odd(piece, cin).reshape(-1, cin).T, flat, preferred_element_type=jnp.float32)
            parts_list.append(jnp.stack([d_odd, d_pair[:cin], d_pair[cin:]], 0))
    return jnp.stack(parts_list, 0).reshape(3, 3, 3, cin, cout)

def reference(features, occupancy, kernel, upstream):
    cin = kernel.shape[3]
    in_mask = expand(occupancy, BE, BE // 2).astype(jnp.bfloat16)[..., None]
    out_mask = expand(occupancy, BE // 2, BE // 2).astype(jnp.bfloat16)[..., None]
    active = features * in_mask
    ext = jnp.pad(active, ((1, 0), (1, 0), (0, 0), (0, 0)))
    coarse = (convolve(ext, kernel) * out_mask.astype(jnp.float32)).astype(jnp.bfloat16)
    grad = upstream * out_mask
    dext = data_grad(kernel, grad)
    feature_grad = (dext[1:, 1:] * in_mask.astype(jnp.float32)).astype(jnp.bfloat16)
    kernel_grad = weight_grad(ext, grad, cin)
    return (coarse, feature_grad, kernel_grad)
```

```python
import jax
import jax.numpy as jnp
from jax import lax
from jax.experimental import pallas as pl
from jax.experimental.pallas import tpu as pltpu
from jax.sharding import PartitionSpec as P

MESH = pl.DeviceIdType.MESH
F32 = jnp.float32
BF16 = jnp.bfloat16
HALF = 864
CHUNK = 16
PEERS = 63


def coordinates():
    gz, gy = lax.axis_index("gz"), lax.axis_index("gy")
    return gz // 8, gy, (gz // 2) % 4, gz % 2


def far_first(t):
    return jnp.where(t == 0, 2, jnp.where(t == 1, 1, jnp.where(t == 2, 3, 0)))


def peer(k, sign):
    x, y, z, c = coordinates()
    px = (x + sign * far_first(k // 16) + 4) % 4
    py = (y + sign * far_first((k // 4) % 4) + 4) % 4
    pz = (z + sign * far_first(k % 4) + 4) % 4
    return px * 16 + py * 4 + pz, ((px * 4 + pz) * 2 + c, py)


def chunk_row(j):
    return ((j * 106) // 63) * 8


def remote(src, dst, send, recv, device):
    return pltpu.make_async_remote_copy(
        src_ref=src, dst_ref=dst, send_sem=send, recv_sem=recv, device_id=device, device_id_type=MESH
    )


def kernel_body(
    feat, occ, ker, ups, coarse, fgrad, kgrad,
    fv, gp, wv, mask, wide, gwt, wf, wd, acc,
    fz_s, fy_s, fz_r, fy_r, fc_r, gz_r, gy_r, gc_r,
    pair_r, rs_r, ag, ag_x, co_v, fg_v, kg_v,
    in_sem, hs_sem, hr_sem, pair_sem, rs_sem, ag_sem, out_sem,
):
    gz, gy = lax.axis_index("gz"), lax.axis_index("gy")
    x, y, z, c = coordinates()
    me = x * 16 + y * 4 + z
    other = (gz + 1 - 2 * c, gy)
    up, down = (gz + 1) % 32, (gz + 31) % 32
    nxt, prv = (gy + 1) % 4, (gy + 3) % 4

    copies = [
        pltpu.make_async_copy(ups, gp.at[0:8, 0:8], in_sem.at[0]),
        pltpu.make_async_copy(feat, fv, in_sem.at[1]),
        pltpu.make_async_copy(ker, wv, in_sem.at[2]),
    ]
    for copy in copies:
        copy.start()

    barrier = pltpu.get_barrier_semaphore()
    for device in ((up, gy), (down, gy), (gz, nxt), (gz, prv), (up, nxt), (down, prv)):
        pl.semaphore_signal(barrier, inc=1, device_id=device, device_id_type=MESH)

    def greet(k, _):
        pl.semaphore_signal(barrier, inc=1, device_id=peer(k, 1)[1], device_id_type=MESH)
        return 0

    lax.fori_loop(0, PEERS, greet, 0)

    pair = lax.broadcasted_iota(jnp.int32, (256, 128), 0) % 32
    held = jnp.zeros((256, 128), jnp.int32)
    for k in range(4):
        held = jnp.where(pair // 8 == k, occ[0, 0, k], held)
    mask[...] = held.astype(F32)
    m32 = held.astype(F32)[:32].astype(BF16)

    copies[2].wait()
    for tap in range(9):
        kz, ky = tap // 3, tap % 3
        rows = slice(tap * 128, tap * 128 + 128)
        left = jnp.concatenate([wv[kz, ky, 1], wv[kz, ky, 2]], 0)
        right = jnp.concatenate([jnp.zeros((64, 128), BF16), wv[kz, ky, 0]], 0)
        wf[rows, 0:128] = left
        wf[rows, 128:256] = right
        wd[rows, 0:128] = left.astype(F32).T.astype(BF16)
        wd[rows, 128:256] = right.astype(F32).T.astype(BF16)

    copies[0].wait()

    def mask_grad(a, _):
        held_g = gp[a, 0:8] * m32[None]
        gp[a, 0:8] = held_g
        flat = held_g.reshape(256, 128).astype(F32)
        later = jnp.where(pair == 31, 0.0, pltpu.roll(flat, 255, 0))
        lanes = pl.ds(pl.multiple_of(a * 256, 256), 256)
        gwt[0:128, lanes] = flat.T.astype(BF16)
        gwt[128:256, lanes] = later.T.astype(BF16)
        return 0

    lax.fori_loop(0, 8, mask_grad, 0)

    copies[1].wait()
    fz_s[...] = fv[15] * m32[None]
    fy_s[...] = fv[:, 15] * m32[None]

    def widen(a, first):
        for kz in range(3):
            for ky in range(3):
                for b in range(8):
                    if (first and kz == 0) or (ky == 0 and b == 0):
                        continue
                    rows = pl.ds(pl.multiple_of(a * 256 + b * 32, 32), 32)
                    tap = kz * 3 + ky
                    wide[rows, tap * 128 : tap * 128 + 128] = fv[2 * a - 1 + kz, 2 * b - 1 + ky] * m32

    widen(0, True)

    def widen_later(a, _):
        widen(a, False)
        return 0

    lax.fori_loop(1, 8, widen_later, 0)

    pl.semaphore_wait(barrier, 6 + PEERS)

    halos = [
        remote(fz_s, fz_r, hs_sem.at[0], hr_sem.at[0], (up, gy)),
        remote(fy_s, fy_r, hs_sem.at[1], hr_sem.at[1], (gz, nxt)),
        remote(fz_s.at[15], fc_r, hs_sem.at[2], hr_sem.at[2], (up, nxt)),
        remote(gp.at[0, 0:8], gz_r, hs_sem.at[3], hr_sem.at[3], (down, gy)),
        remote(gp.at[0:8, 0], gy_r, hs_sem.at[4], hr_sem.at[4], (gz, prv)),
        remote(gp.at[0, 0], gc_r, hs_sem.at[5], hr_sem.at[5], (down, prv)),
    ]
    for copy in halos:
        copy.start()
    for copy in halos[:3]:
        copy.wait_recv()

    has_z = jnp.where(gz > 0, 1.0, 0.0) * jnp.ones((32, 128), F32)
    has_y = jnp.where(gy > 0, 1.0, 0.0) * jnp.ones((32, 128), F32)
    z_on, y_on, c_on = has_z.astype(BF16), has_y.astype(BF16), (has_z * has_y).astype(BF16)
    for ky in range(3):
        for b in range(8):
            row = 2 * b - 1 + ky
            rim = fc_r[...] * c_on if row < 0 else fz_r[row] * z_on
            wide[b * 32 : b * 32 + 32, ky * 128 : ky * 128 + 128] = rim
    for a in range(8):
        for kz in range(3):
            plane = 2 * a - 1 + kz
            if plane >= 0:
                wide[a * 256 : a * 256 + 32, kz * 384 : kz * 384 + 128] = fy_r[plane] * y_on

    for first in range(0, 9, 2):
        taps = range(first, min(first + 2, 9))
        out = jnp.dot(
            gwt[...], wide[:, first * 128 : (taps[-1] + 1) * 128], preferred_element_type=F32
        )
        for tap in taps:
            piece = out[:, (tap - first) * 128 : (tap - first) * 128 + 128]
            acc[tap * 192 + 64 : tap * 192 + 192] = piece[:128].T
            acc[tap * 192 : tap * 192 + 64] = piece[128:].T[64:]

    mine = pl.multiple_of(c * HALF, 8)
    theirs = pl.multiple_of((1 - c) * HALF, 8)
    swap = remote(acc.at[pl.ds(theirs, HALF)], pair_r, pair_sem.at[0], pair_sem.at[1], other)
    swap.start()
    swap.wait_recv()
    acc[pl.ds(mine, HALF)] = acc[pl.ds(mine, HALF)] + pair_r[...]

    def scatter(k, _):
        j, device = peer(k, 1)
        row = pl.multiple_of(c * HALF + chunk_row(j), 8)
        remote(acc.at[pl.ds(row, CHUNK)], rs_r.at[k], rs_sem.at[0], rs_sem.at[1], device).start()
        return 0

    lax.fori_loop(0, PEERS, scatter, 0)

    for copy in halos[3:]:
        copy.wait_recv()
    for copy in halos:
        copy.wait_send()
    last_z = (jnp.where(gz < 31, 1.0, 0.0) * jnp.ones((32, 128), F32))
    last_y = (jnp.where(gy < 3, 1.0, 0.0) * jnp.ones((32, 128), F32))
    gp[8, 0:8] = gz_r[...] * last_z.astype(BF16)[None]
    gp[0:8, 8] = gy_r[...] * last_y.astype(BF16)[None]
    gp[8, 8] = gc_r[...] * (last_z * last_y).astype(BF16)

    def tap_rows(kz, ky):
        return wd[(kz * 3 + ky) * 128 : (kz * 3 + ky) * 128 + 128]

    def back(a, _):
        here = [gp[a + i, j : j + 8].reshape(256, 128) for i in range(2) for j in range(2)]
        for ez in range(2):
            for ey in range(2):
                lhs, rhs = [], []
                for i in range(1 + ez):
                    for j in range(1 + ey):
                        kz = 1 if ez == 0 else 2 - 2 * i
                        ky = 1 if ey == 0 else 2 - 2 * j
                        lhs.append(here[i * 2 + j])
                        rhs.append(tap_rows(kz, ky))
                d = jnp.dot(
                    jnp.concatenate(lhs, 1), jnp.concatenate(rhs, 0), preferred_element_type=F32
                )
                late = jnp.where(pair == 31, 0.0, pltpu.roll(d[:, 128:], 255, 0))
                out = ((d[:, :128] + late) * mask[...]).astype(BF16)
                for b in range(8):
                    fg_v[2 * a + ez, 2 * b + ey] = out[b * 32 : b * 32 + 32]
        return 0

    lax.fori_loop(0, 8, back, 0)
    fg_out = pltpu.make_async_copy(fg_v, fgrad, out_sem.at[0])
    fg_out.start()

    pltpu.make_async_copy(rs_r, rs_r, rs_sem.at[1]).wait()
    own = acc[pl.ds(pl.multiple_of(c * HALF + chunk_row(me), 8), CHUNK)]
    total = lax.fori_loop(0, PEERS, lambda k, t: t + rs_r[k], own)
    ag[me] = total.astype(BF16)

    def gather(k, _):
        remote(ag.at[me], ag.at[me], ag_sem.at[0], ag_sem.at[1], peer(k, 1)[1]).start()
        return 0

    lax.fori_loop(0, PEERS, gather, 0)

    def forward(a, _):
        rows = pl.ds(pl.multiple_of(a * 256, 256), 256)
        d = jnp.dot(wide[rows, :], wf[...], preferred_element_type=F32)
        late = jnp.where(pair == 0, 0.0, pltpu.roll(d[:, 128:], 1, 0))
        co_v[a] = ((d[:, :128] + late) * mask[...]).astype(BF16).reshape(8, 32, 128)
        return 0

    lax.fori_loop(0, 8, forward, 0)
    co_out = pltpu.make_async_copy(co_v, coarse, out_sem.at[1])
    co_out.start()

    pltpu.make_async_copy(ag.at[0:PEERS], ag.at[0:PEERS], ag_sem.at[1]).wait()
    trade = remote(ag, ag_x, pair_sem.at[2], pair_sem.at[3], other)
    trade.start()

    def place(buffer, base):
        def put(j, _):
            row = pl.multiple_of(base + chunk_row(j), 8)
            kg_v[pl.ds(row, CHUNK)] = buffer[j].astype(F32)
            return 0

        lax.fori_loop(0, 64, put, 0)

    place(ag, mine)
    trade.wait_recv()
    place(ag_x, theirs)
    kg_out = pltpu.make_async_copy(kg_v, kgrad, out_sem.at[2])
    kg_out.start()

    swap.wait_send()
    trade.wait_send()
    pltpu.make_async_copy(rs_r, rs_r, rs_sem.at[0]).wait()
    pltpu.make_async_copy(ag.at[0:PEERS], ag.at[0:PEERS], ag_sem.at[0]).wait()
    fg_out.wait()
    co_out.wait()
    kg_out.wait()


def shards(features, occupancy, kernel, upstream):
    vm = pltpu.VMEM
    dma = pltpu.SemaphoreType.DMA
    any_space = pl.BlockSpec(memory_space=pl.ANY)
    coarse, fgrad, kgrad = pl.pallas_call(
        kernel_body,
        out_shape=(
            jax.ShapeDtypeStruct((8, 8, 32, 128), BF16),
            jax.ShapeDtypeStruct((16, 16, 32, 128), BF16),
            jax.ShapeDtypeStruct((1728, 128), F32),
        ),
        in_specs=[any_space, pl.BlockSpec(memory_space=pltpu.SMEM), any_space, any_space],
        out_specs=(any_space, any_space, any_space),
        scratch_shapes=[
            vm((16, 16, 32, 128), BF16),
            vm((9, 9, 32, 128), BF16),
            vm((3, 3, 3, 64, 128), BF16),
            vm((256, 128), F32),
            vm((2048, 1152), BF16),
            vm((256, 2048), BF16),
            vm((1152, 256), BF16),
            vm((1152, 256), BF16),
            vm((1728, 128), F32),
            vm((16, 32, 128), BF16),
            vm((16, 32, 128), BF16),
            vm((16, 32, 128), BF16),
            vm((16, 32, 128), BF16),
            vm((32, 128), BF16),
            vm((8, 32, 128), BF16),
            vm((8, 32, 128), BF16),
            vm((32, 128), BF16),
            vm((HALF, 128), F32),
            vm((PEERS, CHUNK, 128), F32),
            vm((64, CHUNK, 128), BF16),
            vm((64, CHUNK, 128), BF16),
            vm((8, 8, 32, 128), BF16),
            vm((16, 16, 32, 128), BF16),
            vm((1728, 128), F32),
            dma((3,)),
            dma((6,)),
            dma((6,)),
            dma((4,)),
            dma((2,)),
            dma((2,)),
            dma((3,)),
        ],
        compiler_params=pltpu.CompilerParams(
            collective_id=0, has_side_effects=True, vmem_limit_bytes=48 * 1024 * 1024
        ),
    )(features, occupancy, kernel, upstream)
    return coarse, fgrad, kgrad.reshape(3, 3, 3, 64, 128)


def solution(mesh):
    whole = P("gz", "gy", None, None)
    return jax.shard_map(
        shards,
        mesh=mesh,
        in_specs=(whole, P("gz", "gy", None), P(), whole),
        out_specs=(whole, whole, P()),
        check_vma=False,
    )
```

```python
import jax
import jax.numpy as jnp
from jax import lax
from jax.experimental import pallas as pl
from jax.experimental.pallas import tpu as pltpu
from jax.sharding import PartitionSpec as P

MESH = pl.DeviceIdType.MESH
F32 = jnp.float32
BF16 = jnp.bfloat16
HALF = 864
CHUNK = 16
PEERS = 63


def coordinates():
    gz, gy = lax.axis_index("gz"), lax.axis_index("gy")
    return gz // 8, gy, (gz // 2) % 4, gz % 2


def far_first(t):
    return jnp.where(t == 0, 2, jnp.where(t == 1, 1, jnp.where(t == 2, 3, 0)))


def peer(k, sign):
    x, y, z, c = coordinates()
    px = (x + sign * far_first(k // 16) + 4) % 4
    py = (y + sign * far_first((k // 4) % 4) + 4) % 4
    pz = (z + sign * far_first(k % 4) + 4) % 4
    return px * 16 + py * 4 + pz, ((px * 4 + pz) * 2 + c, py)


def chunk_row(j):
    return ((j * 106) // 63) * 8


def remote(src, dst, send, recv, device):
    return pltpu.make_async_remote_copy(
        src_ref=src, dst_ref=dst, send_sem=send, recv_sem=recv, device_id=device, device_id_type=MESH
    )


def kernel_body(
    feat, occ, ker, ups, coarse, fgrad, kgrad,
    fv, gp, wv, mask, wide, gwt, wf, wd, acc,
    fz_s, fy_s, fz_r, fy_r, fc_r, gz_r, gy_r, gc_r,
    pair_r, rs_r, ag, ag_x, co_v, fg_v, kg_v,
    gwy, rim_y, know, in_sem, hs_sem, hr_sem, pair_sem, rs_sem, ag_sem, out_sem,
):
    gz, gy = lax.axis_index("gz"), lax.axis_index("gy")
    x, y, z, c = coordinates()
    me = x * 16 + y * 4 + z
    other = (gz + 1 - 2 * c, gy)
    up, down = (gz + 1) % 32, (gz + 31) % 32
    nxt, prv = (gy + 1) % 4, (gy + 3) % 4

    copies = [
        pltpu.make_async_copy(ups, gp.at[0:8, 0:8], in_sem.at[0]),
        pltpu.make_async_copy(feat, fv, in_sem.at[1]),
        pltpu.make_async_copy(ker, wv, in_sem.at[2]),
    ]
    for copy in copies:
        copy.start()

    barrier = pltpu.get_barrier_semaphore()
    along_x = [((((x + i) % 4) * 4 + z) * 2 + c, gy) for i in (2, 1, 3)]
    along_y = [(gz, (gy + i) % 4) for i in (2, 1, 3)]
    along_z = [((x * 4 + (z + i) % 4) * 2 + c, gy) for i in (2, 1, 3)]
    beside = [(up, nxt), (down, prv), (up, gy), (down, gy)]
    for device in beside + along_y + along_x + along_z:
        pl.semaphore_signal(barrier, inc=1, device_id=device, device_id_type=MESH)

    pair = lax.broadcasted_iota(jnp.int32, (256, 128), 0) % 32
    held = jnp.zeros((256, 128), jnp.int32)
    for k in range(4):
        held = jnp.where(pair // 8 == k, occ[0, 0, k], held)
    mask[...] = held.astype(F32)
    m32 = held.astype(F32)[:32].astype(BF16)

    copies[0].wait()

    def mask_grad(a, _):
        gp[a, 0:8] = gp[a, 0:8] * m32[None]
        return 0

    lax.fori_loop(0, 8, mask_grad, 0)
    copies[1].wait()
    fz_s[...] = fv[15] * m32[None]
    fy_s[...] = fv[:, 15] * m32[None]

    pl.semaphore_wait(barrier, 13)

    halos = [
        remote(fz_s, fz_r, hs_sem.at[0], hr_sem.at[0], (up, gy)),
        remote(fy_s, fy_r, hs_sem.at[1], hr_sem.at[1], (gz, nxt)),
        remote(fz_s.at[15], fc_r, hs_sem.at[2], hr_sem.at[2], (up, nxt)),
        remote(gp.at[0, 0:8], gz_r, hs_sem.at[3], hr_sem.at[3], (down, gy)),
        remote(gp.at[0:8, 0], gy_r, hs_sem.at[4], hr_sem.at[4], (gz, prv)),
        remote(gp.at[0, 0], gc_r, hs_sem.at[5], hr_sem.at[5], (down, prv)),
    ]
    for copy in halos:
        copy.start()
    for device in along_y:
        pl.semaphore_signal(know.at[0], inc=1, device_id=device, device_id_type=MESH)

    def turn(rows, ref, first):
        flat = rows.reshape(256, 128).astype(F32)
        later = jnp.where(pair == 31, 0.0, pltpu.roll(flat, 255, 0))
        lanes = pl.ds(first if isinstance(first, int) else pl.multiple_of(first, 256), 256)
        ref[0:128, lanes] = flat.T.astype(BF16)
        ref[128:256, lanes] = later.T.astype(BF16)

    def turn_plane(a, _):
        turn(gp[a, 0:8], gwt, a * 256)
        return 0

    lax.fori_loop(0, 8, turn_plane, 0)
    turn(gp[0:8, 0], gwy, 0)

    def widen(a, first):
        for kz in range(3):
            for ky in range(3):
                tap = kz * 3 + ky
                for b in range(8):
                    rows = pl.ds(pl.multiple_of(a * 256 + b * 32, 32), 32)
                    if (first and kz == 0) or (ky == 0 and b == 0):
                        piece = jnp.zeros((32, 128), BF16)
                    else:
                        piece = fv[2 * a - 1 + kz, 2 * b - 1 + ky] * m32
                    wide[rows, tap * 128 : tap * 128 + 128] = piece

    widen(0, True)

    def widen_later(a, _):
        widen(a, False)
        return 0

    lax.fori_loop(1, 8, widen_later, 0)

    for first in range(0, 9, 2):
        taps = range(first, min(first + 2, 9))
        out = jnp.dot(
            gwt[...], wide[:, first * 128 : (taps[-1] + 1) * 128], preferred_element_type=F32
        )
        for tap in taps:
            piece = out[:, (tap - first) * 128 : (tap - first) * 128 + 128]
            acc[tap * 192 + 64 : tap * 192 + 192] = piece[:128].T
            acc[tap * 192 : tap * 192 + 64] = piece[128:].T[64:]

    pl.semaphore_wait(know.at[0], 3)
    for device in along_x:
        pl.semaphore_signal(know.at[1], inc=1, device_id=device, device_id_type=MESH)

    for copy in halos[:3]:
        copy.wait_recv()

    has_z = jnp.where(gz > 0, 1.0, 0.0) * jnp.ones((32, 128), F32)
    has_y = jnp.where(gy > 0, 1.0, 0.0) * jnp.ones((32, 128), F32)
    z_on, y_on, c_on = has_z.astype(BF16), has_y.astype(BF16), (has_z * has_y).astype(BF16)
    for ky in range(3):
        for b in range(8):
            row = 2 * b - 1 + ky
            rim = fc_r[...] * c_on if row < 0 else fz_r[row] * z_on
            wide[b * 32 : b * 32 + 32, ky * 128 : ky * 128 + 128] = rim
    for a in range(8):
        for kz in range(3):
            plane = 2 * a - 1 + kz
            rim = fy_r[plane] * y_on if plane >= 0 else jnp.zeros((32, 128), BF16)
            rim_y[a * 32 : a * 32 + 32, kz * 128 : kz * 128 + 128] = rim
            if plane >= 0:
                wide[a * 256 : a * 256 + 32, kz * 384 : kz * 384 + 128] = rim
    by_z = jnp.dot(gwt[:, 0:256], wide[0:256, 0:384], preferred_element_type=F32)
    by_y = jnp.dot(gwy[...], rim_y[...], preferred_element_type=F32)
    for tap, terms in ((0, by_z), (1, by_z), (2, by_z), (0, by_y), (3, by_y), (6, by_y)):
        at = tap if terms is by_z else tap // 3
        piece = terms[:, at * 128 : at * 128 + 128]
        acc[tap * 192 + 64 : tap * 192 + 192] += piece[:128].T
        acc[tap * 192 : tap * 192 + 64] += piece[128:].T[64:]

    mine = pl.multiple_of(c * HALF, 8)
    theirs = pl.multiple_of((1 - c) * HALF, 8)
    swap = remote(acc.at[pl.ds(theirs, HALF)], pair_r, pair_sem.at[0], pair_sem.at[1], other)
    swap.start()
    swap.wait_recv()
    acc[pl.ds(mine, HALF)] = acc[pl.ds(mine, HALF)] + pair_r[...]

    pl.semaphore_wait(know.at[1], 3)

    def scatter(k, _):
        j, device = peer(k, 1)
        row = pl.multiple_of(c * HALF + chunk_row(j), 8)
        remote(acc.at[pl.ds(row, CHUNK)], rs_r.at[k], rs_sem.at[0], rs_sem.at[1], device).start()
        return 0

    lax.fori_loop(0, PEERS, scatter, 0)

    copies[2].wait()
    for tap in range(9):
        kz, ky = tap // 3, tap % 3
        rows = slice(tap * 128, tap * 128 + 128)
        left = jnp.concatenate([wv[kz, ky, 1], wv[kz, ky, 2]], 0)
        right = jnp.concatenate([jnp.zeros((64, 128), BF16), wv[kz, ky, 0]], 0)
        wf[rows, 0:128] = left
        wf[rows, 128:256] = right
        wd[rows, 0:128] = left.astype(F32).T.astype(BF16)
        wd[rows, 128:256] = right.astype(F32).T.astype(BF16)

    for copy in halos[3:]:
        copy.wait_recv()
    for copy in halos:
        copy.wait_send()
    last_z = (jnp.where(gz < 31, 1.0, 0.0) * jnp.ones((32, 128), F32))
    last_y = (jnp.where(gy < 3, 1.0, 0.0) * jnp.ones((32, 128), F32))
    gp[8, 0:8] = gz_r[...] * last_z.astype(BF16)[None]
    gp[0:8, 8] = gy_r[...] * last_y.astype(BF16)[None]
    gp[8, 8] = gc_r[...] * (last_z * last_y).astype(BF16)

    def tap_rows(kz, ky):
        return wd[(kz * 3 + ky) * 128 : (kz * 3 + ky) * 128 + 128]

    def back(a, _):
        here = [gp[a + i, j : j + 8].reshape(256, 128) for i in range(2) for j in range(2)]
        for ez in range(2):
            for ey in range(2):
                lhs, rhs = [], []
                for i in range(1 + ez):
                    for j in range(1 + ey):
                        kz = 1 if ez == 0 else 2 - 2 * i
                        ky = 1 if ey == 0 else 2 - 2 * j
                        lhs.append(here[i * 2 + j])
                        rhs.append(tap_rows(kz, ky))
                d = jnp.dot(
                    jnp.concatenate(lhs, 1), jnp.concatenate(rhs, 0), preferred_element_type=F32
                )
                late = jnp.where(pair == 31, 0.0, pltpu.roll(d[:, 128:], 255, 0))
                out = ((d[:, :128] + late) * mask[...]).astype(BF16)
                for b in range(8):
                    fg_v[2 * a + ez, 2 * b + ey] = out[b * 32 : b * 32 + 32]
        return 0

    lax.fori_loop(0, 8, back, 0)
    fg_out = pltpu.make_async_copy(fg_v, fgrad, out_sem.at[0])
    fg_out.start()

    pltpu.make_async_copy(rs_r, rs_r, rs_sem.at[1]).wait()
    own = acc[pl.ds(pl.multiple_of(c * HALF + chunk_row(me), 8), CHUNK)]
    total = lax.fori_loop(0, PEERS, lambda k, t: t + rs_r[k], own)
    ag[me] = total.astype(BF16)

    def gather(k, _):
        remote(ag.at[me], ag.at[me], ag_sem.at[0], ag_sem.at[1], peer(k, 1)[1]).start()
        return 0

    lax.fori_loop(0, PEERS, gather, 0)

    def forward(a, _):
        rows = pl.ds(pl.multiple_of(a * 256, 256), 256)
        d = jnp.dot(wide[rows, :], wf[...], preferred_element_type=F32)
        late = jnp.where(pair == 0, 0.0, pltpu.roll(d[:, 128:], 1, 0))
        co_v[a] = ((d[:, :128] + late) * mask[...]).astype(BF16).reshape(8, 32, 128)
        return 0

    lax.fori_loop(0, 8, forward, 0)
    co_out = pltpu.make_async_copy(co_v, coarse, out_sem.at[1])
    co_out.start()

    pltpu.make_async_copy(ag.at[0:PEERS], ag.at[0:PEERS], ag_sem.at[1]).wait()
    trade = remote(ag, ag_x, pair_sem.at[2], pair_sem.at[3], other)
    trade.start()

    def place(buffer, base):
        def put(j, _):
            row = pl.multiple_of(base + chunk_row(j), 8)
            kg_v[pl.ds(row, CHUNK)] = buffer[j].astype(F32)
            return 0

        lax.fori_loop(0, 64, put, 0)

    place(ag, mine)
    trade.wait_recv()
    place(ag_x, theirs)
    kg_out = pltpu.make_async_copy(kg_v, kgrad, out_sem.at[2])
    kg_out.start()

    swap.wait_send()
    trade.wait_send()
    pltpu.make_async_copy(rs_r, rs_r, rs_sem.at[0]).wait()
    pltpu.make_async_copy(ag.at[0:PEERS], ag.at[0:PEERS], ag_sem.at[0]).wait()
    fg_out.wait()
    co_out.wait()
    kg_out.wait()


def shards(features, occupancy, kernel, upstream):
    vm = pltpu.VMEM
    dma = pltpu.SemaphoreType.DMA
    any_space = pl.BlockSpec(memory_space=pl.ANY)
    hbm = pl.BlockSpec(memory_space=pltpu.HBM)
    coarse, fgrad, kgrad = pl.pallas_call(
        kernel_body,
        out_shape=(
            jax.ShapeDtypeStruct((8, 8, 32, 128), BF16),
            jax.ShapeDtypeStruct((16, 16, 32, 128), BF16),
            jax.ShapeDtypeStruct((1728, 128), F32),
        ),
        in_specs=[hbm, pl.BlockSpec(memory_space=pltpu.SMEM), hbm, hbm],
        out_specs=(any_space, any_space, any_space),
        scratch_shapes=[
            vm((16, 16, 32, 128), BF16),
            vm((9, 9, 32, 128), BF16),
            vm((3, 3, 3, 64, 128), BF16),
            vm((256, 128), F32),
            vm((2048, 1152), BF16),
            vm((256, 2048), BF16),
            vm((1152, 256), BF16),
            vm((1152, 256), BF16),
            vm((1728, 128), F32),
            vm((16, 32, 128), BF16),
            vm((16, 32, 128), BF16),
            vm((16, 32, 128), BF16),
            vm((16, 32, 128), BF16),
            vm((32, 128), BF16),
            vm((8, 32, 128), BF16),
            vm((8, 32, 128), BF16),
            vm((32, 128), BF16),
            vm((HALF, 128), F32),
            vm((PEERS, CHUNK, 128), F32),
            vm((64, CHUNK, 128), BF16),
            vm((64, CHUNK, 128), BF16),
            vm((8, 8, 32, 128), BF16),
            vm((16, 16, 32, 128), BF16),
            vm((1728, 128), F32),
            vm((256, 256), BF16),
            vm((256, 384), BF16),
            pltpu.SemaphoreType.REGULAR((2,)),
            dma((3,)),
            dma((6,)),
            dma((6,)),
            dma((4,)),
            dma((2,)),
            dma((2,)),
            dma((3,)),
        ],
        compiler_params=pltpu.CompilerParams(
            collective_id=0, has_side_effects=True, vmem_limit_bytes=48 * 1024 * 1024
        ),
    )(features, occupancy, kernel, upstream)
    return coarse, fgrad, kgrad.reshape(3, 3, 3, 64, 128)


def solution(mesh):
    whole = P("gz", "gy", None, None)
    return jax.shard_map(
        shards,
        mesh=mesh,
        in_specs=(whole, P("gz", "gy", None), P(), whole),
        out_specs=(whole, whole, P()),
        check_vma=False,
    )
```

```python
import jax
import jax.numpy as jnp
from jax import lax
from jax.experimental import pallas as pl
from jax.experimental.pallas import tpu as pltpu
from jax.sharding import PartitionSpec as P

MESH = pl.DeviceIdType.MESH
F32 = jnp.float32
BF16 = jnp.bfloat16
HALF = 864
CHUNK = 16
PEERS = 63


def coordinates():
    gz, gy = lax.axis_index("gz"), lax.axis_index("gy")
    return gz // 8, gy, (gz // 2) % 4, gz % 2


def far_first(t):
    return jnp.where(t == 0, 2, jnp.where(t == 1, 1, jnp.where(t == 2, 3, 0)))


def peer(k):
    x, y, z, c = coordinates()
    px = (x + far_first(k >> 4)) & 3
    py = (y + far_first((k >> 2) & 3)) & 3
    pz = (z + far_first(k & 3)) & 3
    return px * 16 + py * 4 + pz, ((px * 4 + pz) * 2 + c, py)


def chunk_row(j):
    return ((j * 106) // 63) * 8


def remote(src, dst, send, recv, device):
    return pltpu.make_async_remote_copy(
        src_ref=src, dst_ref=dst, send_sem=send, recv_sem=recv, device_id=device, device_id_type=MESH
    )


def kernel_body(
    feat, occ_h, ker, ups, coarse, fgrad, ag, ag_x,
    fv, gp, wv, mask, wide, gwt, wf, wd, acc,
    fz_s, fy_s, fz_r, fy_r, fc_r, gz_r, gy_r, gc_r,
    pair_r, rs_r, co_v, fg_v, occ, gwz, rim_z,
    gwy, rim_y, know, in_sem, hs_sem, hr_sem, pair_sem, rs_sem, ag_sem, out_sem,
):
    gz, gy = lax.axis_index("gz"), lax.axis_index("gy")
    x, y, z, c = coordinates()
    me = x * 16 + y * 4 + z
    other = (gz + 1 - 2 * c, gy)
    up, down = (gz + 1) % 32, (gz + 31) % 32
    nxt, prv = (gy + 1) % 4, (gy + 3) % 4

    copies = [
        pltpu.make_async_copy(ups, gp.at[0:8, 0:8], in_sem.at[0]),
        pltpu.make_async_copy(feat, fv, in_sem.at[1]),
        pltpu.make_async_copy(ker, wv, in_sem.at[2]),
        pltpu.make_async_copy(occ_h, occ, in_sem.at[3]),
    ]
    for copy in copies:
        copy.start()

    barrier = pltpu.get_barrier_semaphore()
    along_x = [((((x + i) % 4) * 4 + z) * 2 + c, gy) for i in (2, 1, 3)]
    along_y = [(gz, (gy + i) % 4) for i in (2, 1, 3)]
    along_z = [((x * 4 + (z + i) % 4) * 2 + c, gy) for i in (2, 1, 3)]
    beside = [(up, nxt), (down, prv), (up, gy), (down, gy)]
    for device in beside + along_y + along_x + along_z:
        pl.semaphore_signal(barrier, inc=1, device_id=device, device_id_type=MESH)

    pair = lax.broadcasted_iota(jnp.int32, (256, 128), 0) % 32
    held = jnp.zeros((256, 128), jnp.int32)
    copies[3].wait()
    for k in range(4):
        held = jnp.where(pair // 8 == k, occ[0, 0, k], held)
    mask[...] = held.astype(F32)
    m32 = held.astype(F32)[:32].astype(BF16)

    copies[0].wait()

    def mask_grad(a, _):
        gp[a, 0:8] = gp[a, 0:8] * m32[None]
        return 0

    lax.fori_loop(0, 8, mask_grad, 0)
    copies[1].wait()
    fz_s[...] = fv[15] * m32[None]
    fy_s[...] = fv[:, 15] * m32[None]

    copies[2].wait()
    for tap in range(9):
        kz, ky = tap // 3, tap % 3
        rows = slice(tap * 128, tap * 128 + 128)
        left = jnp.concatenate([wv[kz, ky, 1], wv[kz, ky, 2]], 0)
        right = jnp.concatenate([jnp.zeros((64, 128), BF16), wv[kz, ky, 0]], 0)
        wf[rows, 0:128] = left
        wf[rows, 128:256] = right
        wd[rows, 0:128] = left.astype(F32).T.astype(BF16)
        wd[rows, 128:256] = right.astype(F32).T.astype(BF16)

    def turn(rows, ref, first):
        flat = rows.reshape(-1, 128).astype(F32)
        count = flat.shape[0]
        later = jnp.where(pair[:count] == 31, 0.0, pltpu.roll(flat, count - 1, 0))
        lanes = pl.ds(first if isinstance(first, int) else pl.multiple_of(first, 256), count)
        ref[0:128, lanes] = flat.T.astype(BF16)
        ref[128:256, lanes] = later.T.astype(BF16)

    def turn_plane(a, _):
        turn(gp[a, 0:8], gwt, a * 256)
        return 0

    lax.fori_loop(0, 8, turn_plane, 0)
    for ky in range(3):
        for b in range(12):
            row = 2 * b - 1 + ky
            edge = fz_s[row] if 0 <= row < 16 else jnp.zeros((32, 128), BF16)
            rim_z[b * 32 : b * 32 + 32, ky * 128 : ky * 128 + 128] = edge
    for kz in range(3):
        for a in range(8):
            plane = 2 * a - 1 + kz
            edge = fy_s[plane] if plane >= 0 else jnp.zeros((32, 128), BF16)
            rim_y[a * 32 : a * 32 + 32, kz * 128 : kz * 128 + 128] = edge

    def widen(a, first):
        for kz in range(3):
            for ky in range(3):
                tap = kz * 3 + ky
                for b in range(8):
                    rows = pl.ds(pl.multiple_of(a * 256 + b * 32, 32), 32)
                    if (first and kz == 0) or (ky == 0 and b == 0):
                        piece = jnp.zeros((32, 128), BF16)
                    else:
                        piece = fv[2 * a - 1 + kz, 2 * b - 1 + ky] * m32
                    wide[rows, tap * 128 : tap * 128 + 128] = piece

    widen(0, True)

    def widen_later(a, _):
        widen(a, False)
        return 0

    lax.fori_loop(1, 8, widen_later, 0)

    for first in range(0, 9, 2):
        taps = range(first, min(first + 2, 9))
        out = jnp.dot(
            gwt[...], wide[:, first * 128 : (taps[-1] + 1) * 128], preferred_element_type=F32
        )
        for tap in taps:
            piece = out[:, (tap - first) * 128 : (tap - first) * 128 + 128]
            acc[tap * 192 + 64 : tap * 192 + 192] = piece[:128].T
            acc[tap * 192 : tap * 192 + 64] = piece[128:].T[64:]

    pl.semaphore_wait(barrier, 13)

    halos = [
        remote(gp.at[0, 0], gc_r, hs_sem.at[0], hr_sem.at[0], (down, prv)),
        remote(gp.at[0:8, 0], gy_r, hs_sem.at[1], hr_sem.at[1], (gz, prv)),
        remote(gp.at[0, 0:8], gz_r, hs_sem.at[2], hr_sem.at[2], (down, gy)),
        remote(fy_s, fy_r, hs_sem.at[3], hr_sem.at[3], (gz, nxt)),
        remote(fz_s, fz_r, hs_sem.at[4], hr_sem.at[4], (up, gy)),
        remote(fz_s.at[15], fc_r, hs_sem.at[5], hr_sem.at[5], (up, nxt)),
    ]
    for copy in halos[:3]:
        copy.start()
    for device in along_y:
        pl.semaphore_signal(know.at[0], inc=1, device_id=device, device_id_type=MESH)
    for copy in halos[3:]:
        copy.start()

    pl.semaphore_wait(know.at[0], 3)
    for device in along_x:
        pl.semaphore_signal(know.at[1], inc=1, device_id=device, device_id_type=MESH)

    for copy in halos[:3]:
        copy.wait_recv()
    last_z = jnp.where(gz < 31, 1.0, 0.0) * jnp.ones((32, 128), F32)
    last_y = jnp.where(gy < 3, 1.0, 0.0) * jnp.ones((32, 128), F32)
    gp[8, 0:8] = gz_r[...] * last_z.astype(BF16)[None]
    gp[0:8, 8] = gy_r[...] * last_y.astype(BF16)[None]
    gp[8, 8] = gc_r[...] * (last_z * last_y).astype(BF16)
    turn(gp[8, 0:8], gwz, 0)
    turn(jnp.concatenate([gp[8, 8], jnp.zeros((96, 128), BF16)], 0), gwz, 256)
    turn(gp[0:8, 8], gwy, 0)
    by_z = jnp.dot(gwz[...], rim_z[...], preferred_element_type=F32)
    by_y = jnp.dot(gwy[...], rim_y[...], preferred_element_type=F32)
    for tap in (0, 1, 2, 3, 6):
        if tap == 0:
            piece = by_z[:, 0:128] + by_y[:, 0:128]
        elif tap < 3:
            piece = by_z[:, tap * 128 : tap * 128 + 128]
        else:
            piece = by_y[:, tap // 3 * 128 : tap // 3 * 128 + 128]
        acc[tap * 192 + 64 : tap * 192 + 192] += piece[:128].T
        acc[tap * 192 : tap * 192 + 64] += piece[128:].T[64:]

    mine = pl.multiple_of(c * HALF, 8)
    theirs = pl.multiple_of((1 - c) * HALF, 8)
    swap = remote(acc.at[pl.ds(theirs, HALF)], pair_r, pair_sem.at[0], pair_sem.at[1], other)
    swap.start()
    swap.wait_recv()
    acc[pl.ds(mine, HALF)] = acc[pl.ds(mine, HALF)] + pair_r[...]

    pl.semaphore_wait(know.at[1], 3)

    def scatter(k, _):
        j, device = peer(k)
        row = pl.multiple_of(c * HALF + chunk_row(j), 8)
        remote(acc.at[pl.ds(row, CHUNK)], rs_r.at[k], rs_sem.at[0], rs_sem.at[1], device).start()
        return 0

    lax.fori_loop(0, PEERS, scatter, 0)

    def tap_rows(kz, ky):
        return wd[(kz * 3 + ky) * 128 : (kz * 3 + ky) * 128 + 128]

    def back(a, _):
        here = [gp[a + i, j : j + 8].reshape(256, 128) for i in range(2) for j in range(2)]
        for ez in range(2):
            for ey in range(2):
                lhs, rhs = [], []
                for i in range(1 + ez):
                    for j in range(1 + ey):
                        kz = 1 if ez == 0 else 2 - 2 * i
                        ky = 1 if ey == 0 else 2 - 2 * j
                        lhs.append(here[i * 2 + j])
                        rhs.append(tap_rows(kz, ky))
                d = jnp.dot(
                    jnp.concatenate(lhs, 1), jnp.concatenate(rhs, 0), preferred_element_type=F32
                )
                late = jnp.where(pair == 31, 0.0, pltpu.roll(d[:, 128:], 255, 0))
                out = ((d[:, :128] + late) * mask[...]).astype(BF16)
                for b in range(8):
                    fg_v[2 * a + ez, 2 * b + ey] = out[b * 32 : b * 32 + 32]
        return 0

    lax.fori_loop(0, 8, back, 0)
    fg_out = pltpu.make_async_copy(fg_v, fgrad, out_sem.at[0])
    fg_out.start()

    for copy in halos[3:]:
        copy.wait_recv()
    for copy in halos:
        copy.wait_send()
    has_z = jnp.where(gz > 0, 1.0, 0.0) * jnp.ones((32, 128), F32)
    has_y = jnp.where(gy > 0, 1.0, 0.0) * jnp.ones((32, 128), F32)
    z_on, y_on, c_on = has_z.astype(BF16), has_y.astype(BF16), (has_z * has_y).astype(BF16)
    for ky in range(3):
        for b in range(8):
            row = 2 * b - 1 + ky
            rim = fc_r[...] * c_on if row < 0 else fz_r[row] * z_on
            wide[b * 32 : b * 32 + 32, ky * 128 : ky * 128 + 128] = rim
    for a in range(8):
        for kz in range(3):
            plane = 2 * a - 1 + kz
            if plane >= 0:
                wide[a * 256 : a * 256 + 32, kz * 384 : kz * 384 + 128] = fy_r[plane] * y_on

    pltpu.make_async_copy(rs_r, rs_r, rs_sem.at[1]).wait()
    own = acc[pl.ds(pl.multiple_of(c * HALF + chunk_row(me), 8), CHUNK)]
    total = lax.fori_loop(0, PEERS, lambda k, t: t + rs_r[k], own)
    ag[me] = total.astype(BF16)

    def gather(k, _):
        remote(ag.at[me], ag.at[me], ag_sem.at[0], ag_sem.at[1], peer(k)[1]).start()
        return 0

    lax.fori_loop(0, PEERS, gather, 0)

    def forward(a, _):
        rows = pl.ds(pl.multiple_of(a * 256, 256), 256)
        d = jnp.dot(wide[rows, :], wf[...], preferred_element_type=F32)
        late = jnp.where(pair == 0, 0.0, pltpu.roll(d[:, 128:], 1, 0))
        co_v[a] = ((d[:, :128] + late) * mask[...]).astype(BF16).reshape(8, 32, 128)
        return 0

    lax.fori_loop(0, 8, forward, 0)
    co_out = pltpu.make_async_copy(co_v, coarse, out_sem.at[1])
    co_out.start()

    pltpu.make_async_copy(ag.at[0:PEERS], ag.at[0:PEERS], ag_sem.at[1]).wait()
    trade = remote(ag, ag_x, pair_sem.at[2], pair_sem.at[3], other)
    trade.start()

    trade.wait_recv()
    swap.wait_send()
    trade.wait_send()
    pltpu.make_async_copy(rs_r, rs_r, rs_sem.at[0]).wait()
    pltpu.make_async_copy(ag.at[0:PEERS], ag.at[0:PEERS], ag_sem.at[0]).wait()
    fg_out.wait()
    co_out.wait()


def finish_body(coarse, fgrad, ag, ag_x, coarse_out, fgrad_out, kgrad_out, kg_v, sem):
    first = pltpu.make_async_copy(fgrad, fgrad_out, sem.at[0])
    second = pltpu.make_async_copy(coarse, coarse_out, sem.at[1])
    first.start()
    second.start()
    c = lax.axis_index("gz") & 1
    for buffer, half in ((ag, c), (ag_x, 1 - c)):
        for j in range(64):
            row = pl.multiple_of(half * HALF + chunk_row(j), 8)
            kg_v[pl.ds(row, CHUNK)] = buffer[j].astype(F32)
    third = pltpu.make_async_copy(kg_v, kgrad_out, sem.at[2])
    third.start()
    first.wait()
    second.wait()
    third.wait()


def shards(features, occupancy, kernel, upstream):
    vm = pltpu.VMEM
    dma = pltpu.SemaphoreType.DMA
    any_space = pl.BlockSpec(memory_space=pl.ANY)
    in_vmem = pl.BlockSpec(memory_space=pltpu.VMEM)
    shapes = (
        jax.ShapeDtypeStruct((8, 8, 32, 128), BF16),
        jax.ShapeDtypeStruct((16, 16, 32, 128), BF16),
    )
    gathered = jax.ShapeDtypeStruct((64, CHUNK, 128), BF16)
    arguments = [
        pltpu.with_memory_space_constraint(a, pltpu.HBM)
        for a in (features, occupancy, kernel, upstream)
    ]
    parts = pl.pallas_call(
        kernel_body,
        out_shape=shapes + (gathered, gathered),
        in_specs=[any_space] * 4,
        out_specs=(any_space, any_space, in_vmem, in_vmem),
        scratch_shapes=[
            vm((16, 16, 32, 128), BF16),
            vm((9, 9, 32, 128), BF16),
            vm((3, 3, 3, 64, 128), BF16),
            vm((256, 128), F32),
            vm((2048, 1152), BF16),
            vm((256, 2048), BF16),
            vm((1152, 256), BF16),
            vm((1152, 256), BF16),
            vm((1728, 128), F32),
            vm((16, 32, 128), BF16),
            vm((16, 32, 128), BF16),
            vm((16, 32, 128), BF16),
            vm((16, 32, 128), BF16),
            vm((32, 128), BF16),
            vm((8, 32, 128), BF16),
            vm((8, 32, 128), BF16),
            vm((32, 128), BF16),
            vm((HALF, 128), F32),
            vm((PEERS, CHUNK, 128), F32),
            vm((8, 8, 32, 128), BF16),
            vm((16, 16, 32, 128), BF16),
            pltpu.SMEM((1, 1, 4), jnp.int32),
            vm((256, 384), BF16),
            vm((384, 384), BF16),
            vm((256, 256), BF16),
            vm((256, 384), BF16),
            pltpu.SemaphoreType.REGULAR((2,)),
            dma((4,)),
            dma((6,)),
            dma((6,)),
            dma((4,)),
            dma((2,)),
            dma((2,)),
            dma((2,)),
        ],
        compiler_params=pltpu.CompilerParams(
            collective_id=0, has_side_effects=True, vmem_limit_bytes=48 * 1024 * 1024
        ),
    )(*arguments)
    coarse, fgrad, kgrad = pl.pallas_call(
        finish_body,
        out_shape=shapes + (jax.ShapeDtypeStruct((1728, 128), F32),),
        in_specs=[any_space, any_space, in_vmem, in_vmem],
        out_specs=(any_space,) * 3,
        scratch_shapes=[vm((1728, 128), F32), dma((3,))],
        compiler_params=pltpu.CompilerParams(vmem_limit_bytes=4 * 1024 * 1024),
    )(*parts)
    return coarse, fgrad, kgrad.reshape(3, 3, 3, 64, 128)


def solution(mesh):
    whole = P("gz", "gy", None, None)
    return jax.shard_map(
        shards,
        mesh=mesh,
        in_specs=(whole, P("gz", "gy", None), P(), whole),
        out_specs=(whole, whole, P()),
        check_vma=False,
    )
```

```python
import jax
import jax.numpy as jnp
from jax import lax
from jax.experimental import pallas as pl
from jax.experimental.pallas import tpu as pltpu
from jax.sharding import PartitionSpec as P

MESH = pl.DeviceIdType.MESH
F32 = jnp.float32
BF16 = jnp.bfloat16
HALF = 864
CHUNK = 16
OWNERS = 54
PEERS = 63


def coordinates():
    gz, gy = lax.axis_index("gz"), lax.axis_index("gy")
    return gz // 8, gy, (gz // 2) % 4, gz % 2


def far_first(t):
    return jnp.where(t == 0, 2, jnp.where(t == 1, 1, jnp.where(t == 2, 3, 0)))


def peer(k):
    x, y, z, c = coordinates()
    px = (x + far_first(k >> 4)) & 3
    py = (y + far_first((k >> 2) & 3)) & 3
    pz = (z + far_first(k & 3)) & 3
    return px * 16 + py * 4 + pz, ((px * 4 + pz) * 2 + c, py)


def remote(src, dst, send, recv, device):
    return pltpu.make_async_remote_copy(
        src_ref=src, dst_ref=dst, send_sem=send, recv_sem=recv, device_id=device, device_id_type=MESH
    )


def kernel_body(
    feat, occ_h, ker, ups, coarse, fgrad, ag, ag_x,
    fv, gp, wv, mask, wide, gwt, wf, wd, acc,
    fz_s, fy_s, fz_r, fy_r, fc_r, gz_r, gy_r, gc_r,
    pair_r, rs_r, co_v, fg_v, occ, gwz, rim_z,
    gwy, rim_y, know, in_sem, hs_sem, hr_sem, pair_sem, rs_sem, ag_sem, out_sem,
):
    gz, gy = lax.axis_index("gz"), lax.axis_index("gy")
    x, y, z, c = coordinates()
    me = x * 16 + y * 4 + z
    other = (gz + 1 - 2 * c, gy)
    up, down = (gz + 1) % 32, (gz + 31) % 32
    nxt, prv = (gy + 1) % 4, (gy + 3) % 4

    copies = [
        pltpu.make_async_copy(ups, gp.at[0:8, 0:8], in_sem.at[0]),
        pltpu.make_async_copy(feat, fv, in_sem.at[1]),
        pltpu.make_async_copy(ker, wv, in_sem.at[2]),
        pltpu.make_async_copy(occ_h, occ, in_sem.at[3]),
    ]
    for copy in copies:
        copy.start()

    barrier = pltpu.get_barrier_semaphore()
    along_x = [((((x + i) % 4) * 4 + z) * 2 + c, gy) for i in (2, 1, 3)]
    along_y = [(gz, (gy + i) % 4) for i in (2, 1, 3)]
    along_z = [((x * 4 + (z + i) % 4) * 2 + c, gy) for i in (2, 1, 3)]
    beside = [(up, nxt), (down, prv), (up, gy), (down, gy)]
    for device in beside + along_y + along_x + along_z:
        pl.semaphore_signal(barrier, inc=1, device_id=device, device_id_type=MESH)

    pair = lax.broadcasted_iota(jnp.int32, (256, 128), 0) % 32
    held = jnp.zeros((256, 128), jnp.int32)
    copies[3].wait()
    for k in range(4):
        held = jnp.where(pair // 8 == k, occ[0, 0, k], held)
    mask[...] = held.astype(F32)
    m32 = held.astype(F32)[:32].astype(BF16)

    copies[0].wait()

    def mask_grad(a, _):
        gp[a, 0:8] = gp[a, 0:8] * m32[None]
        return 0

    lax.fori_loop(0, 8, mask_grad, 0)
    pl.semaphore_wait(barrier, 13)

    halos = [
        remote(gp.at[0, 0], gc_r, hs_sem.at[0], hr_sem.at[0], (down, prv)),
        remote(gp.at[0:8, 0], gy_r, hs_sem.at[1], hr_sem.at[1], (gz, prv)),
        remote(gp.at[0, 0:8], gz_r, hs_sem.at[2], hr_sem.at[2], (down, gy)),
        remote(fy_s, fy_r, hs_sem.at[3], hr_sem.at[3], (gz, nxt)),
        remote(fz_s, fz_r, hs_sem.at[4], hr_sem.at[4], (up, gy)),
        remote(fz_s.at[15], fc_r, hs_sem.at[5], hr_sem.at[5], (up, nxt)),
    ]
    for copy in halos[:3]:
        copy.start()
    for device in along_y:
        pl.semaphore_signal(know.at[0], inc=1, device_id=device, device_id_type=MESH)
    copies[1].wait()
    fz_s[...] = fv[15] * m32[None]
    fy_s[...] = fv[:, 15] * m32[None]
    for copy in halos[3:]:
        copy.start()

    copies[2].wait()
    for tap in range(9):
        kz, ky = tap // 3, tap % 3
        rows = slice(tap * 128, tap * 128 + 128)
        left = jnp.concatenate([wv[kz, ky, 1], wv[kz, ky, 2]], 0)
        right = jnp.concatenate([jnp.zeros((64, 128), BF16), wv[kz, ky, 0]], 0)
        wf[rows, 0:128] = left
        wf[rows, 128:256] = right
        wd[rows, 0:128] = left.astype(F32).T.astype(BF16)
        wd[rows, 128:256] = right.astype(F32).T.astype(BF16)

    def turn(rows, ref, first):
        flat = rows.reshape(-1, 128).astype(F32)
        count = flat.shape[0]
        later = jnp.where(pair[:count] == 31, 0.0, pltpu.roll(flat, count - 1, 0))
        lanes = pl.ds(first if isinstance(first, int) else pl.multiple_of(first, 256), count)
        ref[0:128, lanes] = flat.T.astype(BF16)
        ref[128:256, lanes] = later.T.astype(BF16)

    def turn_plane(a, _):
        turn(gp[a, 0:8], gwt, a * 256)
        return 0

    lax.fori_loop(0, 8, turn_plane, 0)
    for ky in range(3):
        for b in range(12):
            row = 2 * b - 1 + ky
            edge = fz_s[row] if 0 <= row < 16 else jnp.zeros((32, 128), BF16)
            rim_z[b * 32 : b * 32 + 32, ky * 128 : ky * 128 + 128] = edge
    for kz in range(3):
        for a in range(8):
            plane = 2 * a - 1 + kz
            edge = fy_s[plane] if plane >= 0 else jnp.zeros((32, 128), BF16)
            rim_y[a * 32 : a * 32 + 32, kz * 128 : kz * 128 + 128] = edge

    def widen(a, first):
        for kz in range(3):
            for ky in range(3):
                tap = kz * 3 + ky
                for b in range(8):
                    rows = pl.ds(pl.multiple_of(a * 256 + b * 32, 32), 32)
                    if (first and kz == 0) or (ky == 0 and b == 0):
                        piece = jnp.zeros((32, 128), BF16)
                    else:
                        piece = fv[2 * a - 1 + kz, 2 * b - 1 + ky] * m32
                    wide[rows, tap * 128 : tap * 128 + 128] = piece

    widen(0, True)

    def widen_later(a, _):
        widen(a, False)
        return 0

    lax.fori_loop(1, 8, widen_later, 0)

    for first in range(0, 9, 2):
        taps = range(first, min(first + 2, 9))
        out = jnp.dot(
            gwt[...], wide[:, first * 128 : (taps[-1] + 1) * 128], preferred_element_type=F32
        )
        for tap in taps:
            piece = out[:, (tap - first) * 128 : (tap - first) * 128 + 128]
            acc[tap * 192 + 64 : tap * 192 + 192] = piece[:128].T
            acc[tap * 192 : tap * 192 + 64] = piece[128:].T[64:]

    pl.semaphore_wait(know.at[0], 3)
    for device in along_x:
        pl.semaphore_signal(know.at[1], inc=1, device_id=device, device_id_type=MESH)

    for copy in halos[:3]:
        copy.wait_recv()
    last_z = jnp.where(gz < 31, 1.0, 0.0) * jnp.ones((32, 128), F32)
    last_y = jnp.where(gy < 3, 1.0, 0.0) * jnp.ones((32, 128), F32)
    gp[8, 0:8] = gz_r[...] * last_z.astype(BF16)[None]
    gp[0:8, 8] = gy_r[...] * last_y.astype(BF16)[None]
    gp[8, 8] = gc_r[...] * (last_z * last_y).astype(BF16)
    turn(gp[8, 0:8], gwz, 0)
    turn(jnp.concatenate([gp[8, 8], jnp.zeros((96, 128), BF16)], 0), gwz, 256)
    turn(gp[0:8, 8], gwy, 0)
    by_z = jnp.dot(gwz[...], rim_z[...], preferred_element_type=F32)
    by_y = jnp.dot(gwy[...], rim_y[...], preferred_element_type=F32)
    for tap in (0, 1, 2, 3, 6):
        if tap == 0:
            piece = by_z[:, 0:128] + by_y[:, 0:128]
        elif tap < 3:
            piece = by_z[:, tap * 128 : tap * 128 + 128]
        else:
            piece = by_y[:, tap // 3 * 128 : tap // 3 * 128 + 128]
        acc[tap * 192 + 64 : tap * 192 + 192] += piece[:128].T
        acc[tap * 192 : tap * 192 + 64] += piece[128:].T[64:]

    mine = pl.multiple_of(c * HALF, 8)
    theirs = pl.multiple_of((1 - c) * HALF, 8)
    swap = remote(acc.at[pl.ds(theirs, HALF)], pair_r, pair_sem.at[0], pair_sem.at[1], other)
    swap.start()
    swap.wait_recv()
    acc[pl.ds(mine, HALF)] = acc[pl.ds(mine, HALF)] + pair_r[...]

    pl.semaphore_wait(know.at[1], 3)

    def scatter(k, _):
        j, device = peer(k)

        @pl.when(j < OWNERS)
        def _():
            row = pl.multiple_of(mine + j * CHUNK, CHUNK)
            remote(acc.at[pl.ds(row, CHUNK)], rs_r.at[k], rs_sem.at[0], rs_sem.at[1], device).start()

        return 0

    lax.fori_loop(0, PEERS, scatter, 0)

    def tap_rows(kz, ky):
        return wd[(kz * 3 + ky) * 128 : (kz * 3 + ky) * 128 + 128]

    def back(a, _):
        here = [gp[a + i, j : j + 8].reshape(256, 128) for i in range(2) for j in range(2)]
        for ez in range(2):
            for ey in range(2):
                lhs, rhs = [], []
                for i in range(1 + ez):
                    for j in range(1 + ey):
                        kz = 1 if ez == 0 else 2 - 2 * i
                        ky = 1 if ey == 0 else 2 - 2 * j
                        lhs.append(here[i * 2 + j])
                        rhs.append(tap_rows(kz, ky))
                d = jnp.dot(
                    jnp.concatenate(lhs, 1), jnp.concatenate(rhs, 0), preferred_element_type=F32
                )
                late = jnp.where(pair == 31, 0.0, pltpu.roll(d[:, 128:], 255, 0))
                out = ((d[:, :128] + late) * mask[...]).astype(BF16)
                for b in range(8):
                    fg_v[2 * a + ez, 2 * b + ey] = out[b * 32 : b * 32 + 32]
        return 0

    lax.fori_loop(0, 8, back, 0)
    fg_out = pltpu.make_async_copy(fg_v, fgrad, out_sem.at[0])
    fg_out.start()

    for copy in halos[3:]:
        copy.wait_recv()
    for copy in halos:
        copy.wait_send()
    has_z = jnp.where(gz > 0, 1.0, 0.0) * jnp.ones((32, 128), F32)
    has_y = jnp.where(gy > 0, 1.0, 0.0) * jnp.ones((32, 128), F32)
    z_on, y_on, c_on = has_z.astype(BF16), has_y.astype(BF16), (has_z * has_y).astype(BF16)
    for ky in range(3):
        for b in range(8):
            row = 2 * b - 1 + ky
            rim = fc_r[...] * c_on if row < 0 else fz_r[row] * z_on
            wide[b * 32 : b * 32 + 32, ky * 128 : ky * 128 + 128] = rim
    for a in range(8):
        for kz in range(3):
            plane = 2 * a - 1 + kz
            if plane >= 0:
                wide[a * 256 : a * 256 + 32, kz * 384 : kz * 384 + 128] = fy_r[plane] * y_on

    def gather(k, _):
        remote(ag.at[me], ag.at[me], ag_sem.at[0], ag_sem.at[1], peer(k)[1]).start()
        return 0

    @pl.when(me < OWNERS)
    def _():
        pltpu.make_async_copy(rs_r, rs_r, rs_sem.at[1]).wait()
        own = acc[pl.ds(pl.multiple_of(mine + me * CHUNK, CHUNK), CHUNK)]
        ag[me] = (own + jnp.sum(rs_r[...], 0)).astype(BF16)
        lax.fori_loop(0, PEERS, gather, 0)

    def forward(a, _):
        rows = pl.ds(pl.multiple_of(a * 256, 256), 256)
        d = jnp.dot(wide[rows, :], wf[...], preferred_element_type=F32)
        late = jnp.where(pair == 0, 0.0, pltpu.roll(d[:, 128:], 1, 0))
        co_v[a] = ((d[:, :128] + late) * mask[...]).astype(BF16).reshape(8, 32, 128)
        return 0

    lax.fori_loop(0, 8, forward, 0)
    co_out = pltpu.make_async_copy(co_v, coarse, out_sem.at[1])
    co_out.start()

    @pl.when(me < OWNERS)
    def _():
        pltpu.make_async_copy(ag.at[1:OWNERS], ag.at[1:OWNERS], ag_sem.at[1]).wait()

    @pl.when(me >= OWNERS)
    def _():
        pltpu.make_async_copy(ag, ag, ag_sem.at[1]).wait()

    trade = remote(ag, ag_x, pair_sem.at[2], pair_sem.at[3], other)
    trade.start()

    trade.wait_recv()
    swap.wait_send()
    trade.wait_send()

    @pl.when(me < OWNERS)
    def _():
        sent = rs_r.at[1:OWNERS]
        pltpu.make_async_copy(sent, sent, rs_sem.at[0]).wait()
        for part in (ag, ag.at[1 : PEERS - OWNERS + 1]):
            pltpu.make_async_copy(part, part, ag_sem.at[0]).wait()

    @pl.when(me >= OWNERS)
    def _():
        sent = rs_r.at[0:OWNERS]
        pltpu.make_async_copy(sent, sent, rs_sem.at[0]).wait()

    fg_out.wait()
    co_out.wait()


def finish_body(coarse, fgrad, ag, ag_x, coarse_out, fgrad_out, kgrad_out, kg_v, sem):
    first = pltpu.make_async_copy(fgrad, fgrad_out, sem.at[0])
    second = pltpu.make_async_copy(coarse, coarse_out, sem.at[1])
    first.start()
    second.start()
    c = lax.axis_index("gz") & 1
    for buffer, half in ((ag, c), (ag_x, 1 - c)):
        for j in range(OWNERS):
            row = pl.multiple_of(half * HALF + j * CHUNK, CHUNK)
            kg_v[pl.ds(row, CHUNK)] = buffer[j].astype(F32)
    third = pltpu.make_async_copy(kg_v, kgrad_out, sem.at[2])
    third.start()
    first.wait()
    second.wait()
    third.wait()


def shards(features, occupancy, kernel, upstream):
    vm = pltpu.VMEM
    dma = pltpu.SemaphoreType.DMA
    any_space = pl.BlockSpec(memory_space=pl.ANY)
    in_vmem = pl.BlockSpec(memory_space=pltpu.VMEM)
    shapes = (
        jax.ShapeDtypeStruct((8, 8, 32, 128), BF16),
        jax.ShapeDtypeStruct((16, 16, 32, 128), BF16),
    )
    gathered = jax.ShapeDtypeStruct((OWNERS, CHUNK, 128), BF16)
    arguments = [
        pltpu.with_memory_space_constraint(a, pltpu.HBM)
        for a in (features, occupancy, kernel, upstream)
    ]
    parts = pl.pallas_call(
        kernel_body,
        out_shape=shapes + (gathered, gathered),
        in_specs=[any_space] * 4,
        out_specs=(any_space, any_space, in_vmem, in_vmem),
        scratch_shapes=[
            vm((16, 16, 32, 128), BF16),
            vm((9, 9, 32, 128), BF16),
            vm((3, 3, 3, 64, 128), BF16),
            vm((256, 128), F32),
            vm((2048, 1152), BF16),
            vm((256, 2048), BF16),
            vm((1152, 256), BF16),
            vm((1152, 256), BF16),
            vm((1728, 128), F32),
            vm((16, 32, 128), BF16),
            vm((16, 32, 128), BF16),
            vm((16, 32, 128), BF16),
            vm((16, 32, 128), BF16),
            vm((32, 128), BF16),
            vm((8, 32, 128), BF16),
            vm((8, 32, 128), BF16),
            vm((32, 128), BF16),
            vm((HALF, 128), F32),
            vm((PEERS, CHUNK, 128), F32),
            vm((8, 8, 32, 128), BF16),
            vm((16, 16, 32, 128), BF16),
            pltpu.SMEM((1, 1, 4), jnp.int32),
            vm((256, 384), BF16),
            vm((384, 384), BF16),
            vm((256, 256), BF16),
            vm((256, 384), BF16),
            pltpu.SemaphoreType.REGULAR((2,)),
            dma((4,)),
            dma((6,)),
            dma((6,)),
            dma((4,)),
            dma((2,)),
            dma((2,)),
            dma((2,)),
        ],
        compiler_params=pltpu.CompilerParams(
            collective_id=0, has_side_effects=True, vmem_limit_bytes=48 * 1024 * 1024
        ),
    )(*arguments)
    coarse, fgrad, kgrad = pl.pallas_call(
        finish_body,
        out_shape=shapes + (jax.ShapeDtypeStruct((1728, 128), F32),),
        in_specs=[any_space, any_space, in_vmem, in_vmem],
        out_specs=(any_space,) * 3,
        scratch_shapes=[vm((1728, 128), F32), dma((3,))],
        compiler_params=pltpu.CompilerParams(vmem_limit_bytes=4 * 1024 * 1024),
    )(*parts)
    return coarse, fgrad, kgrad.reshape(3, 3, 3, 64, 128)


def solution(mesh):
    whole = P("gz", "gy", None, None)
    return jax.shard_map(
        shards,
        mesh=mesh,
        in_specs=(whole, P("gz", "gy", None), P(), whole),
        out_specs=(whole, whole, P()),
        check_vma=False,
    )
```

```python
import jax
import jax.numpy as jnp
from jax import lax
from jax.experimental import pallas as pl
from jax.experimental.pallas import tpu as pltpu
from jax.sharding import PartitionSpec as P

MESH = pl.DeviceIdType.MESH
F32 = jnp.float32
BF16 = jnp.bfloat16
HALF = 864
EARLY = 384
LATE = 480
CHUNK = 16
OWNERS = 54
PEERS = 63


def coordinates():
    gz, gy = lax.axis_index("gz"), lax.axis_index("gy")
    return gz >> 3, gy, (gz >> 1) & 3, gz & 1


def hops(offset):
    return sum(min(o, 4 - o) for o in offset)


OFFSETS = sorted(
    [(i, j, k) for i in range(4) for j in range(4) for k in range(4) if i + j + k], key=hops, reverse=True
)


def number(x, y, z):
    return ((x * 16 + y * 4 + z) * 37) & 63


def peer(offset):
    x, y, z, c = coordinates()
    px, py, pz = (x + offset[0]) & 3, (y + offset[1]) & 3, (z + offset[2]) & 3
    return number(px, py, pz), ((px * 4 + pz) * 2 + c, py)


def first_row(tap):
    return (4, 5, 0, 1, 2, 3, 6, 7, 8).index(tap) * 192


def remote(src, dst, send, recv, device):
    return pltpu.make_async_remote_copy(
        src_ref=src, dst_ref=dst, send_sem=send, recv_sem=recv, device_id=device, device_id_type=MESH
    )


def kernel_body(
    feat, occ_h, ker, ups, coarse, fgrad, kg,
    fv, gp, wv, mask, wide, gwt, wf, wd, acc,
    fz_s, fy_s, fz_r, fy_r, fc_r, gz_r, gy_r, gc_r,
    pair_r, rs_r, ag, ag_x, co_v, fg_v, occ, gwz, rim_z,
    gwy, rim_y, know, in_sem, hs_sem, hr_sem, pair_sem, rs_sem, ag_sem, out_sem,
):
    gz, gy = lax.axis_index("gz"), lax.axis_index("gy")
    x, y, z, c = coordinates()
    me = number(x, y, z)
    other = (gz + 1 - 2 * c, gy)
    up, down = (gz + 1) % 32, (gz + 31) % 32
    nxt, prv = (gy + 1) % 4, (gy + 3) % 4

    barrier = pltpu.get_barrier_semaphore()
    along_x = [((((x + i) % 4) * 4 + z) * 2 + c, gy) for i in (2, 1, 3)]
    along_y = [(gz, (gy + i) % 4) for i in (2, 1, 3)]
    along_z = [((x * 4 + (z + i) % 4) * 2 + c, gy) for i in (2, 1, 3)]
    beside = [(up, nxt), (down, prv), (up, gy), (down, gy)]
    for device in beside + along_y + along_x + along_z:
        pl.semaphore_signal(barrier, inc=1, device_id=device, device_id_type=MESH)

    copies = [
        pltpu.make_async_copy(ups, gp.at[0:8, 0:8], in_sem.at[0]),
        pltpu.make_async_copy(feat, fv, in_sem.at[1]),
        pltpu.make_async_copy(ker, wv, in_sem.at[2]),
        pltpu.make_async_copy(occ_h, occ, in_sem.at[3]),
    ]
    for copy in copies:
        copy.start()

    pair = lax.broadcasted_iota(jnp.int32, (256, 128), 0) % 32
    held = jnp.zeros((256, 128), jnp.int32)
    copies[3].wait()
    for k in range(4):
        held = jnp.where(pair // 8 == k, occ[0, 0, k], held)
    mask[...] = held.astype(F32)
    m32 = held.astype(F32)[:32].astype(BF16)

    copies[0].wait()

    def mask_grad(a, _):
        gp[a, 0:8] = gp[a, 0:8] * m32[None]
        return 0

    lax.fori_loop(0, 8, mask_grad, 0)
    pl.semaphore_wait(barrier, 13)

    halos = [
        remote(gp.at[0, 0], gc_r, hs_sem.at[0], hr_sem.at[0], (down, prv)),
        remote(gp.at[0:8, 0], gy_r, hs_sem.at[1], hr_sem.at[1], (gz, prv)),
        remote(gp.at[0, 0:8], gz_r, hs_sem.at[2], hr_sem.at[2], (down, gy)),
        remote(fy_s, fy_r, hs_sem.at[3], hr_sem.at[3], (gz, nxt)),
        remote(fz_s, fz_r, hs_sem.at[4], hr_sem.at[4], (up, gy)),
        remote(fz_s.at[15], fc_r, hs_sem.at[5], hr_sem.at[5], (up, nxt)),
    ]
    for copy in halos[:3]:
        copy.start()
    for device in along_y:
        pl.semaphore_signal(know.at[0], inc=1, device_id=device, device_id_type=MESH)
    copies[1].wait()
    fz_s[...] = fv[15] * m32[None]
    fy_s[...] = fv[:, 15] * m32[None]
    for copy in halos[3:]:
        copy.start()

    copies[2].wait()
    for tap in range(9):
        kz, ky = tap // 3, tap % 3
        rows = slice(tap * 128, tap * 128 + 128)
        left = jnp.concatenate([wv[kz, ky, 1], wv[kz, ky, 2]], 0)
        right = jnp.concatenate([jnp.zeros((64, 128), BF16), wv[kz, ky, 0]], 0)
        wf[rows, 0:128] = left
        wf[rows, 128:256] = right
        wd[rows, 0:128] = left.T
        wd[rows, 128:256] = right.T

    def turn(rows, ref, first):
        flat = rows.reshape(-1, 128).astype(F32)
        count = flat.shape[0]
        later = jnp.where(pair[:count] == 31, 0.0, pltpu.roll(flat, count - 1, 0))
        lanes = pl.ds(first if isinstance(first, int) else pl.multiple_of(first, 256), count)
        ref[0:128, lanes] = rows.reshape(-1, 128).T
        ref[128:256, lanes] = later.astype(BF16).T

    def turn_plane(a, _):
        turn(gp[a, 0:8], gwt, a * 256)
        return 0

    lax.fori_loop(0, 8, turn_plane, 0)
    for ky in range(3):
        for b in range(12):
            row = 2 * b - 1 + ky
            edge = fz_s[row] if 0 <= row < 16 else jnp.zeros((32, 128), BF16)
            rim_z[b * 32 : b * 32 + 32, ky * 128 : ky * 128 + 128] = edge
    for kz in range(3):
        for a in range(8):
            plane = 2 * a - 1 + kz
            edge = fy_s[plane] if plane >= 0 else jnp.zeros((32, 128), BF16)
            rim_y[a * 32 : a * 32 + 32, kz * 128 : kz * 128 + 128] = edge

    def widen(a, first):
        for kz in range(3):
            for ky in range(3):
                tap = kz * 3 + ky
                for b in range(8):
                    rows = pl.ds(pl.multiple_of(a * 256 + b * 32, 32), 32)
                    if (first and kz == 0) or (ky == 0 and b == 0):
                        piece = jnp.zeros((32, 128), BF16)
                    else:
                        piece = fv[2 * a - 1 + kz, 2 * b - 1 + ky] * m32
                    wide[rows, tap * 128 : tap * 128 + 128] = piece

    widen(0, True)

    def widen_later(a, _):
        widen(a, False)
        return 0

    lax.fori_loop(1, 8, widen_later, 0)

    for first in range(0, 9, 2):
        taps = range(first, min(first + 2, 9))
        out = jnp.dot(
            gwt[...], wide[:, first * 128 : (taps[-1] + 1) * 128], preferred_element_type=F32
        )
        for tap in taps:
            piece = out[:, (tap - first) * 128 : (tap - first) * 128 + 128]
            acc[first_row(tap) + 64 : first_row(tap) + 192] = piece[:128].T
            acc[first_row(tap) : first_row(tap) + 64] = piece[128:].T[64:]

    soon = remote(
        acc.at[pl.ds(pl.multiple_of((1 - c) * 1344, CHUNK), EARLY)], pair_r.at[0:EARLY],
        pair_sem.at[4], pair_sem.at[5], other,
    )
    soon.start()
    pl.semaphore_wait(know.at[0], 3)
    for device in along_x:
        pl.semaphore_signal(know.at[1], inc=1, device_id=device, device_id_type=MESH)

    for copy in halos[:3]:
        copy.wait_recv()
    last_z = jnp.where(gz < 31, 1.0, 0.0) * jnp.ones((32, 128), F32)
    last_y = jnp.where(gy < 3, 1.0, 0.0) * jnp.ones((32, 128), F32)
    gp[8, 0:8] = gz_r[...] * last_z.astype(BF16)[None]
    gp[0:8, 8] = gy_r[...] * last_y.astype(BF16)[None]
    gp[8, 8] = gc_r[...] * (last_z * last_y).astype(BF16)
    turn(gp[8, 0:8], gwz, 0)
    turn(jnp.concatenate([gp[8, 8], jnp.zeros((96, 128), BF16)], 0), gwz, 256)
    turn(gp[0:8, 8], gwy, 0)
    by_z = jnp.dot(gwz[...], rim_z[...], preferred_element_type=F32)
    by_y = jnp.dot(gwy[...], rim_y[...], preferred_element_type=F32)
    for tap in (0, 1, 2, 3, 6):
        if tap == 0:
            piece = by_z[:, 0:128] + by_y[:, 0:128]
        elif tap < 3:
            piece = by_z[:, tap * 128 : tap * 128 + 128]
        else:
            piece = by_y[:, tap // 3 * 128 : tap // 3 * 128 + 128]
        acc[first_row(tap) + 64 : first_row(tap) + 192] += piece[:128].T
        acc[first_row(tap) : first_row(tap) + 64] += piece[128:].T[64:]

    mine = pl.multiple_of(c * HALF, CHUNK)
    late = pl.multiple_of(EARLY + (1 - c) * LATE, CHUNK)
    swap = remote(
        acc.at[pl.ds(late, LATE)], pair_r.at[EARLY:HALF], pair_sem.at[0], pair_sem.at[1], other
    )
    swap.start()
    soon.wait_recv()
    acc[pl.ds(pl.multiple_of(c * 1344, CHUNK), EARLY)] += pair_r[0:EARLY]
    swap.wait_recv()
    acc[pl.ds(pl.multiple_of(EARLY + c * LATE, CHUNK), LATE)] += pair_r[EARLY:HALF]

    pl.semaphore_wait(know.at[1], 3)

    for k, offset in enumerate(OFFSETS):
        j, device = peer(offset)

        @pl.when(j < OWNERS)
        def _():
            row = pl.multiple_of(mine + j * CHUNK, CHUNK)
            remote(acc.at[pl.ds(row, CHUNK)], rs_r.at[k], rs_sem.at[0], rs_sem.at[1], device).start()

    def tap_rows(kz, ky):
        return wd[(kz * 3 + ky) * 128 : (kz * 3 + ky) * 128 + 128]

    def back(a, _):
        here = [gp[a + i, j : j + 8].reshape(256, 128) for i in range(2) for j in range(2)]
        for ez in range(2):
            for ey in range(2):
                lhs, rhs = [], []
                for i in range(1 + ez):
                    for j in range(1 + ey):
                        kz = 1 if ez == 0 else 2 - 2 * i
                        ky = 1 if ey == 0 else 2 - 2 * j
                        lhs.append(here[i * 2 + j])
                        rhs.append(tap_rows(kz, ky))
                d = jnp.dot(
                    jnp.concatenate(lhs, 1), jnp.concatenate(rhs, 0), preferred_element_type=F32
                )
                late = jnp.where(pair == 31, 0.0, pltpu.roll(d[:, 128:], 255, 0))
                out = ((d[:, :128] + late) * mask[...]).astype(BF16)
                for b in range(8):
                    fg_v[2 * a + ez, 2 * b + ey] = out[b * 32 : b * 32 + 32]
        return 0

    lax.fori_loop(0, 8, back, 0)
    fg_out = pltpu.make_async_copy(fg_v, fgrad, out_sem.at[0])
    fg_out.start()

    for copy in halos[3:]:
        copy.wait_recv()
    for copy in halos:
        copy.wait_send()
    has_z = jnp.where(gz > 0, 1.0, 0.0) * jnp.ones((32, 128), F32)
    has_y = jnp.where(gy > 0, 1.0, 0.0) * jnp.ones((32, 128), F32)
    z_on, y_on, c_on = has_z.astype(BF16), has_y.astype(BF16), (has_z * has_y).astype(BF16)
    for ky in range(3):
        for b in range(8):
            row = 2 * b - 1 + ky
            rim = fc_r[...] * c_on if row < 0 else fz_r[row] * z_on
            wide[b * 32 : b * 32 + 32, ky * 128 : ky * 128 + 128] = rim
    for a in range(8):
        for kz in range(3):
            plane = 2 * a - 1 + kz
            if plane >= 0:
                wide[a * 256 : a * 256 + 32, kz * 384 : kz * 384 + 128] = fy_r[plane] * y_on

    @pl.when(me < OWNERS)
    def _():
        pltpu.make_async_copy(rs_r, rs_r, rs_sem.at[1]).wait()
        own = acc[pl.ds(pl.multiple_of(mine + me * CHUNK, CHUNK), CHUNK)]
        ag[me] = (own + jnp.sum(rs_r[...], 0)).astype(BF16)
        for offset in OFFSETS:
            remote(ag.at[me], ag.at[me], ag_sem.at[0], ag_sem.at[1], peer(offset)[1]).start()

    def forward(a, _):
        rows = pl.ds(pl.multiple_of(a * 256, 256), 256)
        d = jnp.dot(wide[rows, :], wf[...], preferred_element_type=F32)
        late = jnp.where(pair == 0, 0.0, pltpu.roll(d[:, 128:], 1, 0))
        co_v[a] = ((d[:, :128] + late) * mask[...]).astype(BF16).reshape(8, 32, 128)
        return 0

    lax.fori_loop(0, 8, forward, 0)
    co_out = pltpu.make_async_copy(co_v, coarse, out_sem.at[1])
    co_out.start()

    @pl.when(me < OWNERS)
    def _():
        pltpu.make_async_copy(ag.at[1:OWNERS], ag.at[1:OWNERS], ag_sem.at[1]).wait()

    @pl.when(me >= OWNERS)
    def _():
        pltpu.make_async_copy(ag, ag, ag_sem.at[1]).wait()

    trade = remote(ag, ag_x, pair_sem.at[2], pair_sem.at[3], other)
    trade.start()


    def place(buffer, half):
        for j in range(OWNERS):
            row = half * HALF + j * CHUNK
            row = jnp.where(row < 384, row + 768, jnp.where(row < 1152, row - 384, row))
            kg[pl.ds(pl.multiple_of(row, CHUNK), CHUNK)] = buffer[j].astype(F32)

    place(ag, c)
    trade.wait_recv()
    place(ag_x, 1 - c)
    soon.wait_send()
    swap.wait_send()
    trade.wait_send()

    @pl.when(me < OWNERS)
    def _():
        sent = rs_r.at[1:OWNERS]
        pltpu.make_async_copy(sent, sent, rs_sem.at[0]).wait()
        for part in (ag, ag.at[1 : PEERS - OWNERS + 1]):
            pltpu.make_async_copy(part, part, ag_sem.at[0]).wait()

    @pl.when(me >= OWNERS)
    def _():
        sent = rs_r.at[0:OWNERS]
        pltpu.make_async_copy(sent, sent, rs_sem.at[0]).wait()

    fg_out.wait()
    co_out.wait()


def finish_body(*refs):
    sem = refs[6]
    copies = [pltpu.make_async_copy(refs[i], refs[i + 3], sem.at[i]) for i in (1, 2, 0)]
    for copy in copies:
        copy.start()
    for copy in copies:
        copy.wait()


def shards(features, occupancy, kernel, upstream):
    vm = pltpu.VMEM
    dma = pltpu.SemaphoreType.DMA
    any_space = pl.BlockSpec(memory_space=pl.ANY)
    in_vmem = pl.BlockSpec(memory_space=pltpu.VMEM)
    shapes = (
        jax.ShapeDtypeStruct((8, 8, 32, 128), BF16),
        jax.ShapeDtypeStruct((16, 16, 32, 128), BF16),
    )
    summed = jax.ShapeDtypeStruct((1728, 128), F32)
    arguments = [
        pltpu.with_memory_space_constraint(a, pltpu.HBM)
        for a in (features, occupancy, kernel, upstream)
    ]
    parts = pl.pallas_call(
        kernel_body,
        out_shape=shapes + (summed,),
        in_specs=[any_space] * 4,
        out_specs=(any_space, any_space, in_vmem),
        scratch_shapes=[
            vm((16, 16, 32, 128), BF16),
            vm((9, 9, 32, 128), BF16),
            vm((3, 3, 3, 64, 128), BF16),
            vm((256, 128), F32),
            vm((2048, 1152), BF16),
            vm((256, 2048), BF16),
            vm((1152, 256), BF16),
            vm((1152, 256), BF16),
            vm((1728, 128), F32),
            vm((16, 32, 128), BF16),
            vm((16, 32, 128), BF16),
            vm((16, 32, 128), BF16),
            vm((16, 32, 128), BF16),
            vm((32, 128), BF16),
            vm((8, 32, 128), BF16),
            vm((8, 32, 128), BF16),
            vm((32, 128), BF16),
            vm((HALF, 128), F32),
            vm((PEERS, CHUNK, 128), F32),
            vm((OWNERS, CHUNK, 128), BF16),
            vm((OWNERS, CHUNK, 128), BF16),
            vm((8, 8, 32, 128), BF16),
            vm((16, 16, 32, 128), BF16),
            pltpu.SMEM((1, 1, 4), jnp.int32),
            vm((256, 384), BF16),
            vm((384, 384), BF16),
            vm((256, 256), BF16),
            vm((256, 384), BF16),
            pltpu.SemaphoreType.REGULAR((2,)),
            dma((4,)),
            dma((6,)),
            dma((6,)),
            dma((6,)),
            dma((2,)),
            dma((2,)),
            dma((2,)),
        ],
        compiler_params=pltpu.CompilerParams(
            collective_id=0, has_side_effects=True, vmem_limit_bytes=48 * 1024 * 1024
        ),
    )(*arguments)
    coarse, fgrad, kgrad = pl.pallas_call(
        finish_body,
        out_shape=shapes + (summed,),
        in_specs=[any_space] * 3,
        out_specs=(any_space,) * 3,
        scratch_shapes=[dma((3,))],
        compiler_params=pltpu.CompilerParams(vmem_limit_bytes=4 * 1024 * 1024),
    )(*parts)
    return coarse, fgrad, kgrad.reshape(3, 3, 3, 64, 128)


def solution(mesh):
    whole = P("gz", "gy", None, None)
    return jax.shard_map(
        shards,
        mesh=mesh,
        in_specs=(whole, P("gz", "gy", None), P(), whole),
        out_specs=(whole, whole, P()),
        check_vma=False,
    )
```

```python
import jax
import jax.numpy as jnp
from jax import lax
from jax.experimental import pallas as pl
from jax.experimental.pallas import tpu as pltpu
from jax.sharding import PartitionSpec as P

MESH = pl.DeviceIdType.MESH
F32 = jnp.float32
BF16 = jnp.bfloat16
HALF = 864
EARLY = 384
LATE = 480
CHUNK = 16
OWNERS = 54
PEERS = 63


def coordinates():
    gz, gy = lax.axis_index("gz"), lax.axis_index("gy")
    return gz >> 3, gy, (gz >> 1) & 3, gz & 1


def hops(offset):
    return sum(min(o, 4 - o) for o in offset)


OFFSETS = sorted(
    [(i, j, k) for i in range(4) for j in range(4) for k in range(4) if i + j + k], key=hops, reverse=True
)


def number(x, y, z):
    return ((x * 16 + y * 4 + z) * 37) & 63


def peer(offset):
    x, y, z, c = coordinates()
    px, py, pz = (x + offset[0]) & 3, (y + offset[1]) & 3, (z + offset[2]) & 3
    return number(px, py, pz), ((px * 4 + pz) * 2 + c, py)


def first_row(tap):
    return (4, 5, 0, 1, 2, 3, 6, 7, 8).index(tap) * 192


def remote(src, dst, send, recv, device):
    return pltpu.make_async_remote_copy(
        src_ref=src, dst_ref=dst, send_sem=send, recv_sem=recv, device_id=device, device_id_type=MESH
    )


def kernel_body(
    feat, occ_h, ker, ups, coarse, fgrad, kg,
    fv, gp, wv, mask, wide, gwt, wf, wd, acc,
    fz_s, fy_s, fz_r, fy_r, fc_r, gz_r, gy_r, gc_r,
    pair_r, rs_r, ag, ag_x, occ, rim_zt, rim_z,
    rim_yt, rim_y, know, in_sem, hs_sem, hr_sem, pair_sem, rs_sem, ag_sem,
):
    gz, gy = lax.axis_index("gz"), lax.axis_index("gy")
    x, y, z, c = coordinates()
    me = number(x, y, z)
    other = (gz + 1 - 2 * c, gy)
    up, down = (gz + 1) % 32, (gz + 31) % 32
    nxt, prv = (gy + 1) % 4, (gy + 3) % 4

    barrier = pltpu.get_barrier_semaphore()
    along_x = [((((x + i) % 4) * 4 + z) * 2 + c, gy) for i in (2, 1, 3)]
    along_y = [(gz, (gy + i) % 4) for i in (2, 1, 3)]
    along_z = [((x * 4 + (z + i) % 4) * 2 + c, gy) for i in (2, 1, 3)]
    beside = [(up, nxt), (down, prv), (up, gy), (down, gy)]
    for device in beside + along_y + along_x + along_z:
        pl.semaphore_signal(barrier, inc=1, device_id=device, device_id_type=MESH)

    copies = [
        pltpu.make_async_copy(ups, gp.at[0:8, 0:8], in_sem.at[0]),
        pltpu.make_async_copy(feat, fv, in_sem.at[1]),
        pltpu.make_async_copy(ker, wv, in_sem.at[2]),
        pltpu.make_async_copy(occ_h, occ, in_sem.at[3]),
    ]
    for copy in copies:
        copy.start()

    pair = lax.broadcasted_iota(jnp.int32, (256, 128), 0) % 32
    held = jnp.zeros((256, 128), jnp.int32)
    copies[3].wait()
    for k in range(4):
        held = jnp.where(pair // 8 == k, occ[0, 0, k], held)
    mask[...] = held.astype(F32)
    m32 = held.astype(F32)[:32].astype(BF16)

    copies[0].wait()

    def mask_grad(a, _):
        gp[a, 0:8] = gp[a, 0:8] * m32[None]
        return 0

    lax.fori_loop(0, 8, mask_grad, 0)
    pl.semaphore_wait(barrier, 13)

    halos = [
        remote(gp.at[0, 0], gc_r, hs_sem.at[0], hr_sem.at[0], (down, prv)),
        remote(gp.at[0:8, 0], gy_r, hs_sem.at[1], hr_sem.at[1], (gz, prv)),
        remote(gp.at[0, 0:8], gz_r, hs_sem.at[2], hr_sem.at[2], (down, gy)),
        remote(fy_s, fy_r, hs_sem.at[3], hr_sem.at[3], (gz, nxt)),
        remote(fz_s, fz_r, hs_sem.at[4], hr_sem.at[4], (up, gy)),
        remote(fz_s.at[15], fc_r, hs_sem.at[5], hr_sem.at[5], (up, nxt)),
    ]
    for copy in halos[:3]:
        copy.start()
    for device in along_y:
        pl.semaphore_signal(know.at[0], inc=1, device_id=device, device_id_type=MESH)
    copies[1].wait()
    fz_s[...] = fv[15] * m32[None]
    fy_s[...] = fv[:, 15] * m32[None]
    for copy in halos[3:]:
        copy.start()

    copies[2].wait()
    for tap in range(9):
        kz, ky = tap // 3, tap % 3
        rows = slice(tap * 128, tap * 128 + 128)
        left = jnp.concatenate([wv[kz, ky, 1], wv[kz, ky, 2]], 0)
        right = jnp.concatenate([jnp.zeros((64, 128), BF16), wv[kz, ky, 0]], 0)
        wf[rows, 0:128] = left
        wf[rows, 128:256] = right
        wd[rows, 0:128] = left.T
        wd[rows, 128:256] = right.T

    def turn(rows, ref, first):
        flat = rows.reshape(-1, 128).astype(F32)
        count = flat.shape[0]
        later = jnp.where(pair[:count] == 31, 0.0, pltpu.roll(flat, count - 1, 0))
        lanes = pl.ds(first if isinstance(first, int) else pl.multiple_of(first, 256), count)
        ref[0:128, lanes] = rows.reshape(-1, 128).T
        ref[128:256, lanes] = later.astype(BF16).T

    def turn_plane(a, _):
        turn(gp[a, 0:8], gwt, a * 256)
        return 0

    lax.fori_loop(0, 8, turn_plane, 0)
    for ky in range(3):
        for b in range(12):
            row = 2 * b - 1 + ky
            edge = fz_s[row] if 0 <= row < 16 else jnp.zeros((32, 128), BF16)
            rim_z[b * 32 : b * 32 + 32, ky * 128 : ky * 128 + 128] = edge
    for kz in range(3):
        for a in range(8):
            plane = 2 * a - 1 + kz
            edge = fy_s[plane] if plane >= 0 else jnp.zeros((32, 128), BF16)
            rim_y[a * 32 : a * 32 + 32, kz * 128 : kz * 128 + 128] = edge
    rim_zt[...] = rim_z[...].T
    rim_yt[...] = rim_y[...].T

    def widen(a, first):
        for kz in range(3):
            for ky in range(3):
                tap = kz * 3 + ky
                for b in range(8):
                    rows = pl.ds(pl.multiple_of(a * 256 + b * 32, 32), 32)
                    if (first and kz == 0) or (ky == 0 and b == 0):
                        piece = jnp.zeros((32, 128), BF16)
                    else:
                        piece = fv[2 * a - 1 + kz, 2 * b - 1 + ky] * m32
                    wide[rows, tap * 128 : tap * 128 + 128] = piece

    widen(0, True)

    def widen_later(a, _):
        widen(a, False)
        return 0

    lax.fori_loop(1, 8, widen_later, 0)

    for first in range(0, 9, 2):
        taps = range(first, min(first + 2, 9))
        out = jnp.dot(
            gwt[...], wide[:, first * 128 : (taps[-1] + 1) * 128], preferred_element_type=F32
        )
        for tap in taps:
            piece = out[:, (tap - first) * 128 : (tap - first) * 128 + 128]
            acc[first_row(tap) + 64 : first_row(tap) + 192] = piece[:128].T
            acc[first_row(tap) : first_row(tap) + 64] = piece[128:].T[64:]

    soon = remote(
        acc.at[pl.ds(pl.multiple_of((1 - c) * 1344, CHUNK), EARLY)], pair_r.at[0:EARLY],
        pair_sem.at[4], pair_sem.at[5], other,
    )
    soon.start()
    pl.semaphore_wait(know.at[0], 3)
    for device in along_x:
        pl.semaphore_signal(know.at[1], inc=1, device_id=device, device_id_type=MESH)

    for copy in halos[:3]:
        copy.wait_recv()
    last_z = jnp.where(gz < 31, 1.0, 0.0) * jnp.ones((32, 128), F32)
    last_y = jnp.where(gy < 3, 1.0, 0.0) * jnp.ones((32, 128), F32)
    gp[8, 0:8] = gz_r[...] * last_z.astype(BF16)[None]
    gp[0:8, 8] = gy_r[...] * last_y.astype(BF16)[None]
    gp[8, 8] = gc_r[...] * (last_z * last_y).astype(BF16)

    def pairwise(flat):
        place = lax.broadcasted_iota(jnp.int32, flat.shape, 0) % 32
        later = jnp.where(place == 31, 0.0, pltpu.roll(flat.astype(F32), flat.shape[0] - 1, 0))
        return jnp.concatenate([flat, later.astype(BF16)], 1)

    beyond = [gp[8, 0:8].reshape(256, 128), gp[8, 8], jnp.zeros((96, 128), BF16)]
    by_z = jnp.dot(rim_zt[...], pairwise(jnp.concatenate(beyond, 0)), preferred_element_type=F32)
    by_y = jnp.dot(rim_yt[...], pairwise(gp[0:8, 8].reshape(256, 128)), preferred_element_type=F32)
    for tap in (0, 1, 2, 3, 6):
        if tap == 0:
            piece = by_z[0:128] + by_y[0:128]
        elif tap < 3:
            piece = by_z[tap * 128 : tap * 128 + 128]
        else:
            piece = by_y[tap // 3 * 128 : tap // 3 * 128 + 128]
        acc[first_row(tap) + 64 : first_row(tap) + 192] += piece[:, :128]
        acc[first_row(tap) : first_row(tap) + 64] += piece[64:, 128:]

    mine = pl.multiple_of(c * HALF, CHUNK)
    late = pl.multiple_of(EARLY + (1 - c) * LATE, CHUNK)
    swap = remote(
        acc.at[pl.ds(late, LATE)], pair_r.at[EARLY:HALF], pair_sem.at[0], pair_sem.at[1], other
    )
    swap.start()
    soon.wait_recv()
    acc[pl.ds(pl.multiple_of(c * 1344, CHUNK), EARLY)] += pair_r[0:EARLY]
    swap.wait_recv()
    acc[pl.ds(pl.multiple_of(EARLY + c * LATE, CHUNK), LATE)] += pair_r[EARLY:HALF]

    pl.semaphore_wait(know.at[1], 3)

    for k, offset in enumerate(OFFSETS):
        j, device = peer(offset)

        @pl.when(j < OWNERS)
        def _():
            row = pl.multiple_of(mine + j * CHUNK, CHUNK)
            remote(acc.at[pl.ds(row, CHUNK)], rs_r.at[k], rs_sem.at[0], rs_sem.at[1], device).start()

    def tap_rows(kz, ky):
        return wd[(kz * 3 + ky) * 128 : (kz * 3 + ky) * 128 + 128]

    def back(a, _):
        here = [gp[a + i, j : j + 8].reshape(256, 128) for i in range(2) for j in range(2)]
        for ez in range(2):
            for ey in range(2):
                lhs, rhs = [], []
                for i in range(1 + ez):
                    for j in range(1 + ey):
                        kz = 1 if ez == 0 else 2 - 2 * i
                        ky = 1 if ey == 0 else 2 - 2 * j
                        lhs.append(here[i * 2 + j])
                        rhs.append(tap_rows(kz, ky))
                d = jnp.dot(
                    jnp.concatenate(lhs, 1), jnp.concatenate(rhs, 0), preferred_element_type=F32
                )
                late = jnp.where(pair == 31, 0.0, pltpu.roll(d[:, 128:], 255, 0))
                out = ((d[:, :128] + late) * mask[...]).astype(BF16)
                for b in range(8):
                    fgrad[2 * a + ez, 2 * b + ey] = out[b * 32 : b * 32 + 32]
        return 0

    lax.fori_loop(0, 8, back, 0)

    for copy in halos[3:]:
        copy.wait_recv()
    for copy in halos:
        copy.wait_send()
    has_z = jnp.where(gz > 0, 1.0, 0.0) * jnp.ones((32, 128), F32)
    has_y = jnp.where(gy > 0, 1.0, 0.0) * jnp.ones((32, 128), F32)
    z_on, y_on, c_on = has_z.astype(BF16), has_y.astype(BF16), (has_z * has_y).astype(BF16)
    for ky in range(3):
        for b in range(8):
            row = 2 * b - 1 + ky
            rim = fc_r[...] * c_on if row < 0 else fz_r[row] * z_on
            wide[b * 32 : b * 32 + 32, ky * 128 : ky * 128 + 128] = rim
    for a in range(8):
        for kz in range(3):
            plane = 2 * a - 1 + kz
            if plane >= 0:
                wide[a * 256 : a * 256 + 32, kz * 384 : kz * 384 + 128] = fy_r[plane] * y_on

    @pl.when(me < OWNERS)
    def _():
        pltpu.make_async_copy(rs_r, rs_r, rs_sem.at[1]).wait()
        own = acc[pl.ds(pl.multiple_of(mine + me * CHUNK, CHUNK), CHUNK)]
        ag[me] = (own + jnp.sum(rs_r[...], 0)).astype(BF16)
        for offset in OFFSETS:
            remote(ag.at[me], ag.at[me], ag_sem.at[0], ag_sem.at[1], peer(offset)[1]).start()

    def forward(a, _):
        rows = pl.ds(pl.multiple_of(a * 256, 256), 256)
        d = jnp.dot(wide[rows, :], wf[...], preferred_element_type=F32)
        late = jnp.where(pair == 0, 0.0, pltpu.roll(d[:, 128:], 1, 0))
        coarse[a] = ((d[:, :128] + late) * mask[...]).astype(BF16).reshape(8, 32, 128)
        return 0

    lax.fori_loop(0, 8, forward, 0)

    @pl.when(me < OWNERS)
    def _():
        pltpu.make_async_copy(ag.at[1:OWNERS], ag.at[1:OWNERS], ag_sem.at[1]).wait()

    @pl.when(me >= OWNERS)
    def _():
        pltpu.make_async_copy(ag, ag, ag_sem.at[1]).wait()

    trade = remote(ag, ag_x, pair_sem.at[2], pair_sem.at[3], other)
    trade.start()


    def place(buffer, half):
        for j in range(OWNERS):
            row = half * HALF + j * CHUNK
            row = jnp.where(row < 384, row + 768, jnp.where(row < 1152, row - 384, row))
            kg[pl.ds(pl.multiple_of(row, CHUNK), CHUNK)] = buffer[j].astype(F32)

    place(ag, c)
    trade.wait_recv()
    place(ag_x, 1 - c)
    soon.wait_send()
    swap.wait_send()
    trade.wait_send()

    @pl.when(me < OWNERS)
    def _():
        sent = rs_r.at[1:OWNERS]
        pltpu.make_async_copy(sent, sent, rs_sem.at[0]).wait()
        for part in (ag, ag.at[1 : PEERS - OWNERS + 1]):
            pltpu.make_async_copy(part, part, ag_sem.at[0]).wait()

    @pl.when(me >= OWNERS)
    def _():
        sent = rs_r.at[0:OWNERS]
        pltpu.make_async_copy(sent, sent, rs_sem.at[0]).wait()


def finish_body(*refs):
    sem = refs[6]
    copies = [pltpu.make_async_copy(refs[i], refs[i + 3], sem.at[i]) for i in (1, 2, 0)]
    for copy in copies:
        copy.start()
    for copy in copies:
        copy.wait()


def shards(features, occupancy, kernel, upstream):
    vm = pltpu.VMEM
    dma = pltpu.SemaphoreType.DMA
    any_space = pl.BlockSpec(memory_space=pl.ANY)
    in_vmem = pl.BlockSpec(memory_space=pltpu.VMEM)
    shapes = (
        jax.ShapeDtypeStruct((8, 8, 32, 128), BF16),
        jax.ShapeDtypeStruct((16, 16, 32, 128), BF16),
    )
    summed = jax.ShapeDtypeStruct((1728, 128), F32)
    arguments = [
        pltpu.with_memory_space_constraint(a, pltpu.HBM)
        for a in (features, occupancy, kernel, upstream)
    ]
    parts = pl.pallas_call(
        kernel_body,
        out_shape=shapes + (summed,),
        in_specs=[any_space] * 4,
        out_specs=(in_vmem,) * 3,
        scratch_shapes=[
            vm((16, 16, 32, 128), BF16),
            vm((9, 9, 32, 128), BF16),
            vm((3, 3, 3, 64, 128), BF16),
            vm((256, 128), F32),
            vm((2048, 1152), BF16),
            vm((256, 2048), BF16),
            vm((1152, 256), BF16),
            vm((1152, 256), BF16),
            vm((1728, 128), F32),
            vm((16, 32, 128), BF16),
            vm((16, 32, 128), BF16),
            vm((16, 32, 128), BF16),
            vm((16, 32, 128), BF16),
            vm((32, 128), BF16),
            vm((8, 32, 128), BF16),
            vm((8, 32, 128), BF16),
            vm((32, 128), BF16),
            vm((HALF, 128), F32),
            vm((PEERS, CHUNK, 128), F32),
            vm((OWNERS, CHUNK, 128), BF16),
            vm((OWNERS, CHUNK, 128), BF16),
            pltpu.SMEM((1, 1, 4), jnp.int32),
            vm((384, 384), BF16),
            vm((384, 384), BF16),
            vm((384, 256), BF16),
            vm((256, 384), BF16),
            pltpu.SemaphoreType.REGULAR((2,)),
            dma((4,)),
            dma((6,)),
            dma((6,)),
            dma((6,)),
            dma((2,)),
            dma((2,)),
        ],
        compiler_params=pltpu.CompilerParams(
            collective_id=0, has_side_effects=True, vmem_limit_bytes=48 * 1024 * 1024
        ),
    )(*arguments)
    coarse, fgrad, kgrad = pl.pallas_call(
        finish_body,
        out_shape=shapes + (summed,),
        in_specs=[any_space] * 3,
        out_specs=(any_space,) * 3,
        scratch_shapes=[dma((3,))],
        compiler_params=pltpu.CompilerParams(vmem_limit_bytes=4 * 1024 * 1024),
    )(*parts)
    return coarse, fgrad, kgrad.reshape(3, 3, 3, 64, 128)


def solution(mesh):
    whole = P("gz", "gy", None, None)
    return jax.shard_map(
        shards,
        mesh=mesh,
        in_specs=(whole, P("gz", "gy", None), P(), whole),
        out_specs=(whole, whole, P()),
        check_vma=False,
    )
```

```python
import jax
import jax.numpy as jnp
from jax import lax
from jax.experimental import pallas as pl
from jax.experimental.pallas import tpu as pltpu
from jax.sharding import PartitionSpec as P

MESH = pl.DeviceIdType.MESH
F32 = jnp.float32
BF16 = jnp.bfloat16
HALF = 864
EARLY = 384
LATE = 480
CHUNK = 16
OWNERS = 54
PEERS = 63


def coordinates():
    gz, gy = lax.axis_index("gz"), lax.axis_index("gy")
    return gz >> 3, gy, (gz >> 1) & 3, gz & 1


def hops(offset):
    return sum(min(o, 4 - o) for o in offset)


OFFSETS = sorted(
    [(i, j, k) for i in range(4) for j in range(4) for k in range(4) if i + j + k], key=hops, reverse=True
)


def number(x, y, z):
    return number_of(x * 16 + y * 4 + z)


def number_of(place):
    return (place * 37) & 63


def peer(offset):
    x, y, z, c = coordinates()
    px, py, pz = (x + offset[0]) & 3, (y + offset[1]) & 3, (z + offset[2]) & 3
    return number(px, py, pz), ((px * 4 + pz) * 2 + c, py)


def first_row(tap):
    return (4, 5, 0, 1, 2, 3, 6, 7, 8).index(tap) * 192


def remote(src, dst, send, recv, device):
    return pltpu.make_async_remote_copy(
        src_ref=src, dst_ref=dst, send_sem=send, recv_sem=recv, device_id=device, device_id_type=MESH
    )


def kernel_body(
    feat, occ_h, ker, ups, coarse, fgrad, kg,
    fv, gp, wv, mask, wide, gwt, wf, wd, acc,
    fz_s, fy_s, fz_r, fy_r, fc_r, gz_r, gy_r, gc_r,
    pair_r, rs_r, ag, ag_x, occ, rim_zt, rim_z,
    rim_yt, rim_y, know, in_sem, hs_sem, hr_sem, pair_sem, rs_sem, ag_sem, trade_sem,
):
    gz, gy = lax.axis_index("gz"), lax.axis_index("gy")
    x, y, z, c = coordinates()
    me = number(x, y, z)
    slot = x * 16 + y * 4 + z
    other = (gz + 1 - 2 * c, gy)
    up, down = (gz + 1) % 32, (gz + 31) % 32
    nxt, prv = (gy + 1) % 4, (gy + 3) % 4

    barrier = pltpu.get_barrier_semaphore()
    along_x = [((((x + i) % 4) * 4 + z) * 2 + c, gy) for i in (2, 1, 3)]
    along_y = [(gz, (gy + i) % 4) for i in (2, 1, 3)]
    along_z = [((x * 4 + (z + i) % 4) * 2 + c, gy) for i in (2, 1, 3)]
    beside = [(up, nxt), (down, prv), (up, gy), (down, gy)]
    for device in beside + along_y + along_x + along_z:
        pl.semaphore_signal(barrier, inc=1, device_id=device, device_id_type=MESH)

    copies = [
        pltpu.make_async_copy(ups, gp.at[0:8, 0:8], in_sem.at[0]),
        pltpu.make_async_copy(feat, fv, in_sem.at[1]),
        pltpu.make_async_copy(ker, wv, in_sem.at[2]),
        pltpu.make_async_copy(occ_h, occ, in_sem.at[3]),
    ]
    for copy in copies:
        copy.start()

    pair = lax.broadcasted_iota(jnp.int32, (256, 128), 0) % 32
    held = jnp.zeros((256, 128), jnp.int32)
    copies[3].wait()
    for k in range(4):
        held = jnp.where(pair // 8 == k, occ[0, 0, k], held)
    mask[...] = held.astype(F32)
    m32 = held.astype(F32)[:32].astype(BF16)

    copies[0].wait()

    def mask_grad(a, _):
        gp[a, 0:8] = gp[a, 0:8] * m32[None]
        return 0

    lax.fori_loop(0, 8, mask_grad, 0)
    pl.semaphore_wait(barrier, 13)

    halos = [
        remote(gp.at[0, 0], gc_r, hs_sem.at[0], hr_sem.at[0], (down, prv)),
        remote(gp.at[0:8, 0], gy_r, hs_sem.at[1], hr_sem.at[1], (gz, prv)),
        remote(gp.at[0, 0:8], gz_r, hs_sem.at[2], hr_sem.at[2], (down, gy)),
        remote(fy_s, fy_r, hs_sem.at[3], hr_sem.at[3], (gz, nxt)),
        remote(fz_s, fz_r, hs_sem.at[4], hr_sem.at[4], (up, gy)),
        remote(fz_s.at[15], fc_r, hs_sem.at[5], hr_sem.at[5], (up, nxt)),
    ]
    for copy in halos[:3]:
        copy.start()
    for device in along_y:
        pl.semaphore_signal(know.at[0], inc=1, device_id=device, device_id_type=MESH)
    copies[1].wait()
    fz_s[...] = fv[15] * m32[None]
    fy_s[...] = fv[:, 15] * m32[None]
    for copy in halos[3:]:
        copy.start()

    copies[2].wait()
    for tap in range(9):
        kz, ky = tap // 3, tap % 3
        rows = slice(tap * 128, tap * 128 + 128)
        left = jnp.concatenate([wv[kz, ky, 1], wv[kz, ky, 2]], 0)
        right = jnp.concatenate([jnp.zeros((64, 128), BF16), wv[kz, ky, 0]], 0)
        wf[rows, 0:128] = left
        wf[rows, 128:256] = right
        wd[rows, 0:128] = left.T
        wd[rows, 128:256] = right.T

    def turn(rows, ref, first):
        flat = rows.reshape(-1, 128).astype(F32)
        count = flat.shape[0]
        later = jnp.where(pair[:count] == 31, 0.0, pltpu.roll(flat, count - 1, 0))
        lanes = pl.ds(first if isinstance(first, int) else pl.multiple_of(first, 256), count)
        ref[0:128, lanes] = rows.reshape(-1, 128).T
        ref[128:256, lanes] = later.astype(BF16).T

    def turn_plane(a, _):
        turn(gp[a, 0:8], gwt, a * 256)
        return 0

    lax.fori_loop(0, 8, turn_plane, 0)
    for ky in range(3):
        for b in range(12):
            row = 2 * b - 1 + ky
            edge = fz_s[row] if 0 <= row < 16 else jnp.zeros((32, 128), BF16)
            rim_z[b * 32 : b * 32 + 32, ky * 128 : ky * 128 + 128] = edge
    for kz in range(3):
        for a in range(8):
            plane = 2 * a - 1 + kz
            edge = fy_s[plane] if plane >= 0 else jnp.zeros((32, 128), BF16)
            rim_y[a * 32 : a * 32 + 32, kz * 128 : kz * 128 + 128] = edge
    rim_zt[...] = rim_z[...].T
    rim_yt[...] = rim_y[...].T

    def widen(a, first):
        for kz in range(3):
            for ky in range(3):
                tap = kz * 3 + ky
                for b in range(8):
                    rows = pl.ds(pl.multiple_of(a * 256 + b * 32, 32), 32)
                    if (first and kz == 0) or (ky == 0 and b == 0):
                        piece = jnp.zeros((32, 128), BF16)
                    else:
                        piece = fv[2 * a - 1 + kz, 2 * b - 1 + ky] * m32
                    wide[rows, tap * 128 : tap * 128 + 128] = piece

    widen(0, True)

    def widen_later(a, _):
        widen(a, False)
        return 0

    lax.fori_loop(1, 8, widen_later, 0)

    for first in range(0, 9, 2):
        taps = range(first, min(first + 2, 9))
        out = jnp.dot(
            gwt[...], wide[:, first * 128 : (taps[-1] + 1) * 128], preferred_element_type=F32
        )
        for tap in taps:
            piece = out[:, (tap - first) * 128 : (tap - first) * 128 + 128]
            acc[first_row(tap) + 64 : first_row(tap) + 192] = piece[:128].T
            acc[first_row(tap) : first_row(tap) + 64] = piece[128:].T[64:]

    soon = remote(
        acc.at[pl.ds(pl.multiple_of((1 - c) * 1344, CHUNK), EARLY)], pair_r.at[0:EARLY],
        pair_sem.at[4], pair_sem.at[5], other,
    )
    soon.start()
    pl.semaphore_wait(know.at[0], 3)
    for device in along_x:
        pl.semaphore_signal(know.at[1], inc=1, device_id=device, device_id_type=MESH)

    for copy in halos[:3]:
        copy.wait_recv()
    last_z = jnp.where(gz < 31, 1.0, 0.0) * jnp.ones((32, 128), F32)
    last_y = jnp.where(gy < 3, 1.0, 0.0) * jnp.ones((32, 128), F32)
    gp[8, 0:8] = gz_r[...] * last_z.astype(BF16)[None]
    gp[0:8, 8] = gy_r[...] * last_y.astype(BF16)[None]
    gp[8, 8] = gc_r[...] * (last_z * last_y).astype(BF16)

    def pairwise(flat):
        place = lax.broadcasted_iota(jnp.int32, flat.shape, 0) % 32
        later = jnp.where(place == 31, 0.0, pltpu.roll(flat.astype(F32), flat.shape[0] - 1, 0))
        return jnp.concatenate([flat, later.astype(BF16)], 1)

    beyond = [gp[8, 0:8].reshape(256, 128), gp[8, 8], jnp.zeros((96, 128), BF16)]
    by_z = jnp.dot(rim_zt[...], pairwise(jnp.concatenate(beyond, 0)), preferred_element_type=F32)
    by_y = jnp.dot(rim_yt[...], pairwise(gp[0:8, 8].reshape(256, 128)), preferred_element_type=F32)
    for tap in (0, 1, 2, 3, 6):
        if tap == 0:
            piece = by_z[0:128] + by_y[0:128]
        elif tap < 3:
            piece = by_z[tap * 128 : tap * 128 + 128]
        else:
            piece = by_y[tap // 3 * 128 : tap // 3 * 128 + 128]
        acc[first_row(tap) + 64 : first_row(tap) + 192] += piece[:, :128]
        acc[first_row(tap) : first_row(tap) + 64] += piece[64:, 128:]

    mine = pl.multiple_of(c * HALF, CHUNK)
    late = pl.multiple_of(EARLY + (1 - c) * LATE, CHUNK)
    swap = remote(
        acc.at[pl.ds(late, LATE)], pair_r.at[EARLY:HALF], pair_sem.at[0], pair_sem.at[1], other
    )
    swap.start()
    soon.wait_recv()
    acc[pl.ds(pl.multiple_of(c * 1344, CHUNK), EARLY)] += pair_r[0:EARLY]
    swap.wait_recv()
    acc[pl.ds(pl.multiple_of(EARLY + c * LATE, CHUNK), LATE)] += pair_r[EARLY:HALF]

    pl.semaphore_wait(know.at[1], 3)

    for k, offset in enumerate(OFFSETS):
        j, device = peer(offset)

        @pl.when(j < OWNERS)
        def _():
            row = pl.multiple_of(mine + j * CHUNK, CHUNK)
            remote(acc.at[pl.ds(row, CHUNK)], rs_r.at[k], rs_sem.at[0], rs_sem.at[1], device).start()

    def tap_rows(kz, ky):
        return wd[(kz * 3 + ky) * 128 : (kz * 3 + ky) * 128 + 128]

    def back(a, _):
        here = [gp[a + i, j : j + 8].reshape(256, 128) for i in range(2) for j in range(2)]
        for ez in range(2):
            for ey in range(2):
                lhs, rhs = [], []
                for i in range(1 + ez):
                    for j in range(1 + ey):
                        kz = 1 if ez == 0 else 2 - 2 * i
                        ky = 1 if ey == 0 else 2 - 2 * j
                        lhs.append(here[i * 2 + j])
                        rhs.append(tap_rows(kz, ky))
                d = jnp.dot(
                    jnp.concatenate(lhs, 1), jnp.concatenate(rhs, 0), preferred_element_type=F32
                )
                late = jnp.where(pair == 31, 0.0, pltpu.roll(d[:, 128:], 255, 0))
                out = ((d[:, :128] + late) * mask[...]).astype(BF16)
                for b in range(8):
                    fgrad[2 * a + ez, 2 * b + ey] = out[b * 32 : b * 32 + 32]
        return 0

    lax.fori_loop(0, 8, back, 0)

    for copy in halos[3:]:
        copy.wait_recv()
    for copy in halos:
        copy.wait_send()
    has_z = jnp.where(gz > 0, 1.0, 0.0) * jnp.ones((32, 128), F32)
    has_y = jnp.where(gy > 0, 1.0, 0.0) * jnp.ones((32, 128), F32)
    z_on, y_on, c_on = has_z.astype(BF16), has_y.astype(BF16), (has_z * has_y).astype(BF16)
    for ky in range(3):
        for b in range(8):
            row = 2 * b - 1 + ky
            rim = fc_r[...] * c_on if row < 0 else fz_r[row] * z_on
            wide[b * 32 : b * 32 + 32, ky * 128 : ky * 128 + 128] = rim
    for a in range(8):
        for kz in range(3):
            plane = 2 * a - 1 + kz
            if plane >= 0:
                wide[a * 256 : a * 256 + 32, kz * 384 : kz * 384 + 128] = fy_r[plane] * y_on

    @pl.when(me < OWNERS)
    def _():
        pltpu.make_async_copy(rs_r, rs_r, rs_sem.at[1]).wait()
        own = acc[pl.ds(pl.multiple_of(mine + me * CHUNK, CHUNK), CHUNK)]
        ag[slot] = (own + jnp.sum(rs_r[...], 0)).astype(BF16)
        for offset in OFFSETS:
            landed = ag_sem.at[1 + (-offset[0]) % 4]
            remote(ag.at[slot], ag.at[slot], ag_sem.at[0], landed, peer(offset)[1]).start()

    def forward(a, _):
        rows = pl.ds(pl.multiple_of(a * 256, 256), 256)
        d = jnp.dot(wide[rows, :], wf[...], preferred_element_type=F32)
        late = jnp.where(pair == 0, 0.0, pltpu.roll(d[:, 128:], 1, 0))
        coarse[a] = ((d[:, :128] + late) * mask[...]).astype(BF16).reshape(8, 32, 128)
        return 0

    lax.fori_loop(0, 8, forward, 0)

    for place in range(64):
        if number_of(place) >= OWNERS:
            ag[place] = jnp.zeros((CHUNK, 128), BF16)
    trades = {}
    for ahead in (0, 1, 3, 2):
        group = (x + ahead) & 3
        missing = group & 1
        if ahead == 0:
            missing = missing + jnp.where(me < OWNERS, 1, 0)
        for count in (14, 13, 12):

            @pl.when(missing == 14 - count)
            def _():
                part = ag.at[0:count]
                pltpu.make_async_copy(part, part, ag_sem.at[1 + ahead]).wait()

        rows = pl.ds(group * 16, 16)
        trades[ahead] = remote(
            ag.at[rows], ag_x.at[rows], trade_sem.at[ahead], trade_sem.at[4 + ahead], other
        )
        trades[ahead].start()

    def write(buffer, half, places):
        for which in range(2):

            @pl.when(half == which)
            def _():
                for place in places:
                    j = number_of(place)
                    if j < OWNERS:
                        row = which * HALF + j * CHUNK
                        row = row + 768 if row < 384 else row - 384 if row < 1152 else row
                        kg[row : row + CHUNK] = buffer[place].astype(F32)

    write(ag, c, range(64))
    for trade in trades.values():
        trade.wait_recv()
    write(ag_x, 1 - c, range(64))
    soon.wait_send()
    swap.wait_send()
    for trade in trades.values():
        trade.wait_send()

    @pl.when(me < OWNERS)
    def _():
        sent = rs_r.at[1:OWNERS]
        pltpu.make_async_copy(sent, sent, rs_sem.at[0]).wait()
        part = ag.at[0:PEERS]
        pltpu.make_async_copy(part, part, ag_sem.at[0]).wait()

    @pl.when(me >= OWNERS)
    def _():
        sent = rs_r.at[0:OWNERS]
        pltpu.make_async_copy(sent, sent, rs_sem.at[0]).wait()


def finish_body(*refs):
    sem = refs[6]
    copies = [pltpu.make_async_copy(refs[i], refs[i + 3], sem.at[i]) for i in (1, 2, 0)]
    for copy in copies:
        copy.start()
    for copy in copies:
        copy.wait()


def shards(features, occupancy, kernel, upstream):
    vm = pltpu.VMEM
    dma = pltpu.SemaphoreType.DMA
    any_space = pl.BlockSpec(memory_space=pl.ANY)
    in_vmem = pl.BlockSpec(memory_space=pltpu.VMEM)
    shapes = (
        jax.ShapeDtypeStruct((8, 8, 32, 128), BF16),
        jax.ShapeDtypeStruct((16, 16, 32, 128), BF16),
    )
    summed = jax.ShapeDtypeStruct((1728, 128), F32)
    arguments = [
        pltpu.with_memory_space_constraint(a, pltpu.HBM)
        for a in (features, occupancy, kernel, upstream)
    ]
    parts = pl.pallas_call(
        kernel_body,
        out_shape=shapes + (summed,),
        in_specs=[any_space] * 4,
        out_specs=(in_vmem,) * 3,
        scratch_shapes=[
            vm((16, 16, 32, 128), BF16),
            vm((9, 9, 32, 128), BF16),
            vm((3, 3, 3, 64, 128), BF16),
            vm((256, 128), F32),
            vm((2048, 1152), BF16),
            vm((256, 2048), BF16),
            vm((1152, 256), BF16),
            vm((1152, 256), BF16),
            vm((1728, 128), F32),
            vm((16, 32, 128), BF16),
            vm((16, 32, 128), BF16),
            vm((16, 32, 128), BF16),
            vm((16, 32, 128), BF16),
            vm((32, 128), BF16),
            vm((8, 32, 128), BF16),
            vm((8, 32, 128), BF16),
            vm((32, 128), BF16),
            vm((HALF, 128), F32),
            vm((PEERS, CHUNK, 128), F32),
            vm((64, CHUNK, 128), BF16),
            vm((64, CHUNK, 128), BF16),
            pltpu.SMEM((1, 1, 4), jnp.int32),
            vm((384, 384), BF16),
            vm((384, 384), BF16),
            vm((384, 256), BF16),
            vm((256, 384), BF16),
            pltpu.SemaphoreType.REGULAR((2,)),
            dma((4,)),
            dma((6,)),
            dma((6,)),
            dma((6,)),
            dma((2,)),
            dma((5,)),
            dma((8,)),
        ],
        compiler_params=pltpu.CompilerParams(
            collective_id=0, has_side_effects=True, vmem_limit_bytes=48 * 1024 * 1024
        ),
    )(*arguments)
    coarse, fgrad, kgrad = pl.pallas_call(
        finish_body,
        out_shape=shapes + (summed,),
        in_specs=[any_space] * 3,
        out_specs=(any_space,) * 3,
        scratch_shapes=[dma((3,))],
        compiler_params=pltpu.CompilerParams(vmem_limit_bytes=4 * 1024 * 1024),
    )(*parts)
    return coarse, fgrad, kgrad.reshape(3, 3, 3, 64, 128)


def solution(mesh):
    whole = P("gz", "gy", None, None)
    return jax.shard_map(
        shards,
        mesh=mesh,
        in_specs=(whole, P("gz", "gy", None), P(), whole),
        out_specs=(whole, whole, P()),
        check_vma=False,
    )
```

```python
import jax
import jax.numpy as jnp
from jax import lax
from jax.experimental import pallas as pl
from jax.experimental.pallas import tpu as pltpu
from jax.sharding import PartitionSpec as P

MESH = pl.DeviceIdType.MESH
F32 = jnp.float32
BF16 = jnp.bfloat16
HALF = 864
EARLY = 384
LATE = 480
CHUNK = 16
OWNERS = 54
PEERS = 63


def coordinates():
    gz, gy = lax.axis_index("gz"), lax.axis_index("gy")
    return gz >> 3, gy, (gz >> 1) & 3, gz & 1


def hops(offset):
    return sum(min(o, 4 - o) for o in offset)


OFFSETS = sorted(
    [(i, j, k) for i in range(4) for j in range(4) for k in range(4) if i + j + k], key=hops, reverse=True
)


def number(x, y, z):
    return ((x * 16 + y * 4 + z) * 37) & 63


def peer(offset):
    x, y, z, c = coordinates()
    px, py, pz = (x + offset[0]) & 3, (y + offset[1]) & 3, (z + offset[2]) & 3
    return number(px, py, pz), ((px * 4 + pz) * 2 + c, py)


def first_row(tap):
    return (4, 5, 0, 1, 2, 3, 6, 7, 8).index(tap) * 192


def remote(src, dst, send, recv, device):
    return pltpu.make_async_remote_copy(
        src_ref=src, dst_ref=dst, send_sem=send, recv_sem=recv, device_id=device, device_id_type=MESH
    )


def kernel_body(
    feat, occ_h, ker, ups, coarse, fgrad, kg,
    fv, gp, wv, mask, wide, gwt, wf, wd, acc,
    fz_s, fy_s, fz_r, fy_r, fc_r, gz_r, gy_r, gc_r,
    pair_r, rs_r, ag, ag_x, occ, rim_zt, rim_z,
    rim_yt, rim_y, know, in_sem, hs_sem, hr_sem, pair_sem, rs_sem, ag_sem,
):
    gz, gy = lax.axis_index("gz"), lax.axis_index("gy")
    x, y, z, c = coordinates()
    me = number(x, y, z)
    other = (gz + 1 - 2 * c, gy)
    up, down = (gz + 1) % 32, (gz + 31) % 32
    nxt, prv = (gy + 1) % 4, (gy + 3) % 4

    barrier = pltpu.get_barrier_semaphore()
    along_x = [((((x + i) % 4) * 4 + z) * 2 + c, gy) for i in (2, 1, 3)]
    along_y = [(gz, (gy + i) % 4) for i in (2, 1, 3)]
    along_z = [((x * 4 + (z + i) % 4) * 2 + c, gy) for i in (2, 1, 3)]
    beside = [(up, nxt), (down, prv), (up, gy), (down, gy)]
    for device in beside + along_y + along_x + along_z:
        pl.semaphore_signal(barrier, inc=1, device_id=device, device_id_type=MESH)

    copies = [
        pltpu.make_async_copy(ups, gp.at[0:8, 0:8], in_sem.at[0]),
        pltpu.make_async_copy(feat, fv, in_sem.at[1]),
        pltpu.make_async_copy(ker, wv, in_sem.at[2]),
        pltpu.make_async_copy(occ_h, occ, in_sem.at[3]),
    ]
    for copy in copies:
        copy.start()

    pair = lax.broadcasted_iota(jnp.int32, (256, 128), 0) % 32
    held = jnp.zeros((256, 128), jnp.int32)
    copies[3].wait()
    for k in range(4):
        held = jnp.where(pair // 8 == k, occ[0, 0, k], held)
    mask[...] = held.astype(F32)
    m32 = held.astype(F32)[:32].astype(BF16)

    copies[0].wait()

    def mask_grad(a, _):
        gp[a, 0:8] = gp[a, 0:8] * m32[None]
        return 0

    lax.fori_loop(0, 8, mask_grad, 0)
    pl.semaphore_wait(barrier, 13)

    halos = [
        remote(gp.at[0, 0], gc_r, hs_sem.at[0], hr_sem.at[0], (down, prv)),
        remote(gp.at[0:8, 0], gy_r, hs_sem.at[1], hr_sem.at[1], (gz, prv)),
        remote(gp.at[0, 0:8], gz_r, hs_sem.at[2], hr_sem.at[2], (down, gy)),
        remote(fy_s, fy_r, hs_sem.at[3], hr_sem.at[3], (gz, nxt)),
        remote(fz_s, fz_r, hs_sem.at[4], hr_sem.at[4], (up, gy)),
        remote(fz_s.at[15], fc_r, hs_sem.at[5], hr_sem.at[5], (up, nxt)),
    ]
    for copy in halos[:3]:
        copy.start()
    for device in along_y:
        pl.semaphore_signal(know.at[0], inc=1, device_id=device, device_id_type=MESH)
    copies[1].wait()
    fz_s[...] = fv[15] * m32[None]
    fy_s[...] = fv[:, 15] * m32[None]
    for copy in halos[3:]:
        copy.start()

    copies[2].wait()
    for tap in range(9):
        kz, ky = tap // 3, tap % 3
        rows = slice(tap * 128, tap * 128 + 128)
        left = jnp.concatenate([wv[kz, ky, 1], wv[kz, ky, 2]], 0)
        right = jnp.concatenate([jnp.zeros((64, 128), BF16), wv[kz, ky, 0]], 0)
        wf[rows, 0:128] = left
        wf[rows, 128:256] = right
        wd[rows, 0:128] = left.T
        wd[rows, 128:256] = right.T

    def turn(rows, ref, first):
        flat = rows.reshape(-1, 128).astype(F32)
        count = flat.shape[0]
        later = jnp.where(pair[:count] == 31, 0.0, pltpu.roll(flat, count - 1, 0))
        lanes = pl.ds(first if isinstance(first, int) else pl.multiple_of(first, 256), count)
        ref[0:128, lanes] = rows.reshape(-1, 128).T
        ref[128:256, lanes] = later.astype(BF16).T

    def turn_plane(a, _):
        turn(gp[a, 0:8], gwt, a * 256)
        return 0

    lax.fori_loop(0, 8, turn_plane, 0)
    for ky in range(3):
        for b in range(12):
            row = 2 * b - 1 + ky
            edge = fz_s[row] if 0 <= row < 16 else jnp.zeros((32, 128), BF16)
            rim_z[b * 32 : b * 32 + 32, ky * 128 : ky * 128 + 128] = edge
    for kz in range(3):
        for a in range(8):
            plane = 2 * a - 1 + kz
            edge = fy_s[plane] if plane >= 0 else jnp.zeros((32, 128), BF16)
            rim_y[a * 32 : a * 32 + 32, kz * 128 : kz * 128 + 128] = edge
    rim_zt[...] = rim_z[...].T
    rim_yt[...] = rim_y[...].T

    def widen(a, first):
        for kz in range(3):
            for ky in range(3):
                tap = kz * 3 + ky
                for b in range(8):
                    rows = pl.ds(pl.multiple_of(a * 256 + b * 32, 32), 32)
                    if (first and kz == 0) or (ky == 0 and b == 0):
                        piece = jnp.zeros((32, 128), BF16)
                    else:
                        piece = fv[2 * a - 1 + kz, 2 * b - 1 + ky] * m32
                    wide[rows, tap * 128 : tap * 128 + 128] = piece

    widen(0, True)

    def widen_later(a, _):
        widen(a, False)
        return 0

    lax.fori_loop(1, 8, widen_later, 0)

    for first in range(0, 9, 2):
        taps = range(first, min(first + 2, 9))
        out = jnp.dot(
            gwt[...], wide[:, first * 128 : (taps[-1] + 1) * 128], preferred_element_type=F32
        )
        for tap in taps:
            piece = out[:, (tap - first) * 128 : (tap - first) * 128 + 128]
            acc[first_row(tap) + 64 : first_row(tap) + 192] = piece[:128].T
            acc[first_row(tap) : first_row(tap) + 64] = piece[128:].T[64:]

    soon = remote(
        acc.at[pl.ds(pl.multiple_of((1 - c) * 1344, CHUNK), EARLY)], pair_r.at[0:EARLY],
        pair_sem.at[4], pair_sem.at[5], other,
    )
    soon.start()
    pl.semaphore_wait(know.at[0], 3)
    for device in along_x:
        pl.semaphore_signal(know.at[1], inc=1, device_id=device, device_id_type=MESH)

    for copy in halos[:3]:
        copy.wait_recv()
    last_z = jnp.where(gz < 31, 1.0, 0.0) * jnp.ones((32, 128), F32)
    last_y = jnp.where(gy < 3, 1.0, 0.0) * jnp.ones((32, 128), F32)
    gp[8, 0:8] = gz_r[...] * last_z.astype(BF16)[None]
    gp[0:8, 8] = gy_r[...] * last_y.astype(BF16)[None]
    gp[8, 8] = gc_r[...] * (last_z * last_y).astype(BF16)

    def pairwise(flat):
        place = lax.broadcasted_iota(jnp.int32, flat.shape, 0) % 32
        later = jnp.where(place == 31, 0.0, pltpu.roll(flat.astype(F32), flat.shape[0] - 1, 0))
        return jnp.concatenate([flat, later.astype(BF16)], 1)

    beyond = [gp[8, 0:8].reshape(256, 128), gp[8, 8], jnp.zeros((96, 128), BF16)]
    by_z = jnp.dot(rim_zt[...], pairwise(jnp.concatenate(beyond, 0)), preferred_element_type=F32)
    by_y = jnp.dot(rim_yt[...], pairwise(gp[0:8, 8].reshape(256, 128)), preferred_element_type=F32)
    for tap in (0, 1, 2, 3, 6):
        if tap == 0:
            piece = by_z[0:128] + by_y[0:128]
        elif tap < 3:
            piece = by_z[tap * 128 : tap * 128 + 128]
        else:
            piece = by_y[tap // 3 * 128 : tap // 3 * 128 + 128]
        acc[first_row(tap) + 64 : first_row(tap) + 192] += piece[:, :128]
        acc[first_row(tap) : first_row(tap) + 64] += piece[64:, 128:]

    mine = pl.multiple_of(c * HALF, CHUNK)
    late = pl.multiple_of(EARLY + (1 - c) * LATE, CHUNK)
    swap = remote(
        acc.at[pl.ds(late, LATE)], pair_r.at[EARLY:HALF], pair_sem.at[0], pair_sem.at[1], other
    )
    swap.start()
    soon.wait_recv()
    acc[pl.ds(pl.multiple_of(c * 1344, CHUNK), EARLY)] += pair_r[0:EARLY]
    swap.wait_recv()
    acc[pl.ds(pl.multiple_of(EARLY + c * LATE, CHUNK), LATE)] += pair_r[EARLY:HALF]

    pl.semaphore_wait(know.at[1], 3)

    for k, offset in enumerate(OFFSETS):
        j, device = peer(offset)

        @pl.when(j < OWNERS)
        def _():
            row = pl.multiple_of(mine + j * CHUNK, CHUNK)
            remote(acc.at[pl.ds(row, CHUNK)], rs_r.at[k], rs_sem.at[0], rs_sem.at[1], device).start()

    def tap_rows(kz, ky):
        return wd[(kz * 3 + ky) * 128 : (kz * 3 + ky) * 128 + 128]

    def back(a, _):
        here = [gp[a + i, j : j + 8].reshape(256, 128) for i in range(2) for j in range(2)]
        for ez in range(2):
            for ey in range(2):
                lhs, rhs = [], []
                for i in range(1 + ez):
                    for j in range(1 + ey):
                        kz = 1 if ez == 0 else 2 - 2 * i
                        ky = 1 if ey == 0 else 2 - 2 * j
                        lhs.append(here[i * 2 + j])
                        rhs.append(tap_rows(kz, ky))
                d = jnp.dot(
                    jnp.concatenate(lhs, 1), jnp.concatenate(rhs, 0), preferred_element_type=F32
                )
                late = jnp.where(pair == 31, 0.0, pltpu.roll(d[:, 128:], 255, 0))
                out = ((d[:, :128] + late) * mask[...]).astype(BF16)
                for b in range(8):
                    fgrad[2 * a + ez, 2 * b + ey] = out[b * 32 : b * 32 + 32]
        return 0

    lax.fori_loop(0, 8, back, 0)

    for copy in halos[3:]:
        copy.wait_recv()
    for copy in halos:
        copy.wait_send()
    has_z = jnp.where(gz > 0, 1.0, 0.0) * jnp.ones((32, 128), F32)
    has_y = jnp.where(gy > 0, 1.0, 0.0) * jnp.ones((32, 128), F32)
    z_on, y_on, c_on = has_z.astype(BF16), has_y.astype(BF16), (has_z * has_y).astype(BF16)
    for ky in range(3):
        for b in range(8):
            row = 2 * b - 1 + ky
            rim = fc_r[...] * c_on if row < 0 else fz_r[row] * z_on
            wide[b * 32 : b * 32 + 32, ky * 128 : ky * 128 + 128] = rim
    for a in range(8):
        for kz in range(3):
            plane = 2 * a - 1 + kz
            if plane >= 0:
                wide[a * 256 : a * 256 + 32, kz * 384 : kz * 384 + 128] = fy_r[plane] * y_on

    @pl.when(me < OWNERS)
    def _():
        pltpu.make_async_copy(rs_r, rs_r, rs_sem.at[1]).wait()
        own = acc[pl.ds(pl.multiple_of(mine + me * CHUNK, CHUNK), CHUNK)]
        ag[me] = (own + jnp.sum(rs_r[...], 0)).astype(BF16)
        for offset in OFFSETS:
            remote(ag.at[me], ag.at[me], ag_sem.at[0], ag_sem.at[1], peer(offset)[1]).start()

    def forward(a, _):
        rows = pl.ds(pl.multiple_of(a * 256, 256), 256)
        d = jnp.dot(wide[rows, :], wf[...], preferred_element_type=F32)
        late = jnp.where(pair == 0, 0.0, pltpu.roll(d[:, 128:], 1, 0))
        coarse[a] = ((d[:, :128] + late) * mask[...]).astype(BF16).reshape(8, 32, 128)
        return 0

    lax.fori_loop(0, 8, forward, 0)

    @pl.when(me < OWNERS)
    def _():
        pltpu.make_async_copy(ag.at[1:OWNERS], ag.at[1:OWNERS], ag_sem.at[1]).wait()

    @pl.when(me >= OWNERS)
    def _():
        pltpu.make_async_copy(ag, ag, ag_sem.at[1]).wait()

    trade = remote(ag, ag_x, pair_sem.at[2], pair_sem.at[3], other)
    trade.start()


    def place(buffer, half):
        for which in range(2):

            @pl.when(half == which)
            def _():
                for j in range(OWNERS):
                    row = which * HALF + j * CHUNK
                    row = row + 768 if row < 384 else row - 384 if row < 1152 else row
                    kg[row : row + CHUNK] = buffer[j].astype(F32)

    place(ag, c)
    trade.wait_recv()
    place(ag_x, 1 - c)
    soon.wait_send()
    swap.wait_send()
    trade.wait_send()

    @pl.when(me < OWNERS)
    def _():
        sent = rs_r.at[1:OWNERS]
        pltpu.make_async_copy(sent, sent, rs_sem.at[0]).wait()
        for part in (ag, ag.at[1 : PEERS - OWNERS + 1]):
            pltpu.make_async_copy(part, part, ag_sem.at[0]).wait()

    @pl.when(me >= OWNERS)
    def _():
        sent = rs_r.at[0:OWNERS]
        pltpu.make_async_copy(sent, sent, rs_sem.at[0]).wait()


def finish_body(*refs):
    sem = refs[6]
    copies = [pltpu.make_async_copy(refs[i], refs[i + 3], sem.at[i]) for i in (1, 2, 0)]
    for copy in copies:
        copy.start()
    for copy in copies:
        copy.wait()


def shards(features, occupancy, kernel, upstream):
    vm = pltpu.VMEM
    dma = pltpu.SemaphoreType.DMA
    any_space = pl.BlockSpec(memory_space=pl.ANY)
    in_vmem = pl.BlockSpec(memory_space=pltpu.VMEM)
    shapes = (
        jax.ShapeDtypeStruct((8, 8, 32, 128), BF16),
        jax.ShapeDtypeStruct((16, 16, 32, 128), BF16),
    )
    summed = jax.ShapeDtypeStruct((1728, 128), F32)
    arguments = [
        pltpu.with_memory_space_constraint(a, pltpu.HBM)
        for a in (features, occupancy, kernel, upstream)
    ]
    parts = pl.pallas_call(
        kernel_body,
        out_shape=shapes + (summed,),
        in_specs=[any_space] * 4,
        out_specs=(in_vmem,) * 3,
        scratch_shapes=[
            vm((16, 16, 32, 128), BF16),
            vm((9, 9, 32, 128), BF16),
            vm((3, 3, 3, 64, 128), BF16),
            vm((256, 128), F32),
            vm((2048, 1152), BF16),
            vm((256, 2048), BF16),
            vm((1152, 256), BF16),
            vm((1152, 256), BF16),
            vm((1728, 128), F32),
            vm((16, 32, 128), BF16),
            vm((16, 32, 128), BF16),
            vm((16, 32, 128), BF16),
            vm((16, 32, 128), BF16),
            vm((32, 128), BF16),
            vm((8, 32, 128), BF16),
            vm((8, 32, 128), BF16),
            vm((32, 128), BF16),
            vm((HALF, 128), F32),
            vm((PEERS, CHUNK, 128), F32),
            vm((OWNERS, CHUNK, 128), BF16),
            vm((OWNERS, CHUNK, 128), BF16),
            pltpu.SMEM((1, 1, 4), jnp.int32),
            vm((384, 384), BF16),
            vm((384, 384), BF16),
            vm((384, 256), BF16),
            vm((256, 384), BF16),
            pltpu.SemaphoreType.REGULAR((2,)),
            dma((4,)),
            dma((6,)),
            dma((6,)),
            dma((6,)),
            dma((2,)),
            dma((2,)),
        ],
        compiler_params=pltpu.CompilerParams(
            collective_id=0, has_side_effects=True, vmem_limit_bytes=48 * 1024 * 1024
        ),
    )(*arguments)
    coarse, fgrad, kgrad = pl.pallas_call(
        finish_body,
        out_shape=shapes + (summed,),
        in_specs=[any_space] * 3,
        out_specs=(any_space,) * 3,
        scratch_shapes=[dma((3,))],
        compiler_params=pltpu.CompilerParams(vmem_limit_bytes=4 * 1024 * 1024),
    )(*parts)
    return coarse, fgrad, kgrad.reshape(3, 3, 3, 64, 128)


def solution(mesh):
    whole = P("gz", "gy", None, None)
    return jax.shard_map(
        shards,
        mesh=mesh,
        in_specs=(whole, P("gz", "gy", None), P(), whole),
        out_specs=(whole, whole, P()),
        check_vma=False,
    )
```
